1024 devices in a mesh: ctx: 16 (over x_hi, y), dp: 64 (over z, x_lo, core).
Axes of the slice: x: 8 (x_hi: 2, x_lo: 4; x = x_hi * 4 + x_lo), y: 8, z: 8, core: 2. Of those that a mesh axis runs over, the one named last changes fastest.
Arguments:
- queries: bfloat16 [64, 2048, 1024], P('dp', 'ctx'), may hold values from -6 to 6
- keys_in: bfloat16 [64, 2048, 256], P('dp', 'ctx'), may hold values from -6 to 6
- values_in: bfloat16 [64, 2048, 256], P('dp', 'ctx'), may hold values from -6 to 6
- patch_order: int32 [64, 16, 128], P('dp', 'ctx'), may hold values from 0 to 127, each once within a row
- block_mask: int32 [64, 64, 8], P('dp', 'ctx'), may hold values 0 or 1
- out_weight: bfloat16 [1024, 1024], P('dp'), may hold values from -0.1875 to 0.1875
- cotangent: bfloat16 [64, 2048, 1024], P('dp', 'ctx'), may hold values from -6 to 6
Outputs:
- mixed: bfloat16 [64, 2048, 1024], P('dp', 'ctx')
- grad_queries: bfloat16 [64, 2048, 1024], P('dp', 'ctx')
- grad_keys: bfloat16 [64, 2048, 256], P('dp', 'ctx')
- grad_values: bfloat16 [64, 2048, 256], P('dp', 'ctx')
- grad_weight: float32 [1024, 1024], P('dp', 'ctx')
The draws below stay inside these ranges and needn't reach their ends.
Inputs may be any that keep to these rules, and one draw needn't show every extreme that they name: `patch_order`: each row of 128 entries is a permutation.
All inputs are finite; a program needn't handle non-finite values. No bound on the sum of `block_mask` on one device may be relied on, other than what follows from the above.
Results may differ from the reference program's by a relative error of at most 0.015.
Values may be sent and summed in bfloat16 or wider, within the bound.
A program may use at most 32 MiB of HBM per device.

```python
import math
import jax
import jax.numpy as jnp
from jax import lax

D = 1024
QUERY_HEADS = 8
KEY_VALUE_HEADS = 2
HEAD_WIDTH = 128
BLK = 32
TILE_TOKENS = 128
SEQS = 64
LEN = 2048
HW = 1024
KVW = 256
N_CTX = 16


def draw_queries(key, part):
    drawn = jnp.clip(jax.random.normal(jax.random.fold_in(key, 1), (SEQS, LEN, HW), jnp.float32), -4.0, 4.0)
    return drawn.astype(jnp.bfloat16)


def draw_keys_in(key, part):
    drawn = jnp.clip(jax.random.normal(jax.random.fold_in(key, 13), (SEQS, LEN, KVW), jnp.float32), -4.0, 4.0)
    return drawn.astype(jnp.bfloat16)


def touch_ends(values, key, least, high):
    longest = values.shape.index(max(values.shape))
    spots = []
    for shift in (0, 1):
        where = [jax.random.randint(jax.random.fold_in(key, axis), (), 0, length) for axis, length in enumerate(values.shape)]
        where[longest] = (where[longest] + shift) % values.shape[longest]
        spots.append(tuple(where))
    return values.at[spots[0]].set(least).at[spots[1]].set(high)


def steps_of(key, shape, split, smallest, top_value):
    def one(axis_at, blocks):
        draws = jax.random.uniform(jax.random.fold_in(jax.random.fold_in(key, 6), axis_at), (blocks,), jnp.float32, smallest / len(split), top_value / len(split))
        return jnp.repeat(jnp.exp(draws), shape[axis_at] // blocks).reshape((-1,) + (1,) * (len(shape) - axis_at - 1))

    factor_of = one(*split[0])
    for cut in split[1:]:
        factor_of = factor_of * one(*cut)
    return factor_of


def noise(rng, extent, deviation, most, split=(), kind=jnp.bfloat16):
    drawn = jax.random.normal(rng, extent, jnp.float32) * deviation
    if len(split) > 0:
        drawn = steps_of(rng, extent, split, -0.22, 0.18) * drawn
    return jnp.clip(drawn, min=-most, max=most).astype(kind)


def setup_inputs(seed: int = 0) -> dict:
    splits = jax.random.split(jax.random.key(seed), 8)
    queries = draw_queries(jax.random.fold_in(splits[7], 71), 0)
    keys_in = draw_keys_in(jax.random.fold_in(splits[7], 71), 0)
    values_in = noise(splits[2], (SEQS, LEN, KVW), 1.0, 6.0, ((0, 64), (1, 16)))
    patch_order = jax.vmap(lambda own: jax.random.permutation(own, TILE_TOKENS))(jax.random.split(splits[3], SEQS * N_CTX)).reshape((SEQS, N_CTX, TILE_TOKENS)).astype(jnp.int32)
    block_mask = touch_ends((jax.random.randint(splits[4], (SEQS, LEN // BLK, 2 * TILE_TOKENS // BLK), 0, 4) < 3).astype(jnp.int32), jax.random.fold_in(splits[4], 1), 0, 1)
    out_weight = noise(splits[5], (HW, D), HW ** -0.5, 0.1875, ((0, 64),))
    cotangent = noise(splits[6], (SEQS, LEN, D), 1.0, 6.0, ((0, 64), (1, 16)))
    return dict(queries=queries, keys_in=keys_in, values_in=values_in, patch_order=patch_order, block_mask=block_mask, out_weight=out_weight, cotangent=cotangent)


def settle_band(band_parts):
    wide = band_parts.astype(jnp.float32)
    own_part = wide[:, TILE_TOKENS:2 * TILE_TOKENS]
    from_right = jnp.roll(wide[:, :TILE_TOKENS], -1, 0)
    from_left = jnp.roll(wide[:, 2 * TILE_TOKENS:], 1, 0)
    return (own_part + from_right + from_left).astype(jnp.bfloat16).reshape(LEN, KVW)

def reference(queries, keys_in, values_in, patch_order, block_mask, out_weight, cotangent):
    scale = 1.0 / math.sqrt(HEAD_WIDTH)
    query_group = QUERY_HEADS // KEY_VALUE_HEADS

    def one_sequence(carry, inputs):
        query_buffer, key_buffer, value_buffer, order_rows, mask_rows, dy_store = inputs
        offsets = (jnp.arange(N_CTX, dtype=jnp.int32) * TILE_TOKENS)[:, None]
        row_position = (order_rows.astype(jnp.int32) + offsets).reshape(-1).astype(jnp.int32)
        query_sequence = query_buffer[row_position].reshape(N_CTX, TILE_TOKENS, KEY_VALUE_HEADS, query_group, HEAD_WIDTH)
        key_sequence = key_buffer[row_position].reshape(N_CTX, TILE_TOKENS, KEY_VALUE_HEADS, HEAD_WIDTH)
        value_sequence = value_buffer[row_position].reshape(N_CTX, TILE_TOKENS, KEY_VALUE_HEADS, HEAD_WIDTH)
        key_band = jnp.concatenate([jnp.roll(key_sequence, 1, 0), key_sequence, jnp.roll(key_sequence, -1, 0)], 1)
        value_band = jnp.concatenate([jnp.roll(value_sequence, 1, 0), value_sequence, jnp.roll(value_sequence, -1, 0)], 1)
        mask_tiles = mask_rows.reshape(N_CTX, TILE_TOKENS // BLK, 2 * TILE_TOKENS // BLK)
        expanded = jnp.repeat(jnp.repeat(mask_tiles, BLK, 1), BLK, 2) > 0
        allowed = jnp.concatenate([expanded[:, :, :TILE_TOKENS], jnp.ones((N_CTX, TILE_TOKENS, TILE_TOKENS), bool), expanded[:, :, TILE_TOKENS:]], 2)
        allowed = allowed[:, None, None]
        scores = jnp.einsum('ctkgd,cskd->ckgts', query_sequence.astype(jnp.float32), key_band.astype(jnp.float32)) * scale
        scores = jnp.where(allowed, scores, -1e+30)
        highest = lax.optimization_barrier(jnp.max(scores, axis=-1, keepdims=True))
        weights = jnp.where(allowed, jnp.exp(scores - highest), 0.0)
        probs = weights / lax.optimization_barrier(jnp.sum(weights, axis=-1, keepdims=True))
        probs_b = probs.astype(jnp.bfloat16)
        attended_f = jnp.einsum('ckgts,cskd->ctkgd', probs_b.astype(jnp.float32), value_band.astype(jnp.float32))
        attended = attended_f.astype(jnp.bfloat16).reshape(LEN, HW)
        mixed_seq = jnp.dot(attended, out_weight, preferred_element_type=jnp.float32).astype(jnp.bfloat16)
        mixed_out = jnp.zeros((LEN, D), jnp.bfloat16).at[row_position].set(mixed_seq)
        dy_seq = dy_store[row_position]
        attention_gradient = jnp.dot(dy_seq, out_weight.T, preferred_element_type=jnp.float32).astype(jnp.bfloat16)
        grad_part = jnp.dot(attended.T, dy_seq, preferred_element_type=jnp.float32)
        attention_gradient5 = attention_gradient.reshape(N_CTX, TILE_TOKENS, KEY_VALUE_HEADS, query_group, HEAD_WIDTH)
        d_probs = jnp.einsum('ctkgd,cskd->ckgts', attention_gradient5.astype(jnp.float32), value_band.astype(jnp.float32))
        delta = lax.optimization_barrier(jnp.sum(attention_gradient5.astype(jnp.float32) * attended_f, axis=-1))
        delta = jnp.transpose(delta, (0, 2, 3, 1))[..., None]
        d_scores_b = (probs * (d_probs - delta)).astype(jnp.bfloat16)
        grad_q_seq = (jnp.einsum('ckgts,cskd->ctkgd', d_scores_b.astype(jnp.float32), key_band.astype(jnp.float32)) * scale).astype(jnp.bfloat16).reshape(LEN, HW)
        part_k = (jnp.einsum('ckgts,ctkgd->cskd', d_scores_b.astype(jnp.float32), query_sequence.astype(jnp.float32)) * scale).astype(jnp.bfloat16)
        part_v = jnp.einsum('ckgts,ctkgd->cskd', probs_b.astype(jnp.float32), attention_gradient5.astype(jnp.float32)).astype(jnp.bfloat16)
        grad_q_out = jnp.zeros((LEN, HW), jnp.bfloat16).at[row_position].set(grad_q_seq)
        grad_k_out = jnp.zeros((LEN, KVW), jnp.bfloat16).at[row_position].set(settle_band(part_k))
        grad_v_out = jnp.zeros((LEN, KVW), jnp.bfloat16).at[row_position].set(settle_band(part_v))
        return (carry + grad_part, (mixed_out, grad_q_out, grad_k_out, grad_v_out))
    start_total = jnp.zeros((HW, D), jnp.float32)
    total, outputs = lax.scan(one_sequence, start_total, (queries, keys_in, values_in, patch_order, block_mask, cotangent))
    grad_weight = total * (1.0 / math.sqrt(SEQS * LEN))
    return (outputs[0], outputs[1], outputs[2], outputs[3], grad_weight)
```

```python
import functools
import math

import jax
import jax.numpy as jnp
from jax import lax
from jax.experimental import pallas as pl
from jax.experimental.pallas import tpu as pltpu
from jax.sharding import PartitionSpec as P

MESH = pl.DeviceIdType.MESH
BF = jnp.bfloat16
F32 = jnp.float32
HD = 128
T = 128
D = 1024
GROUP = 4
GROUPS = 2
KV = 256
BLK = 32
D7 = (1, -1, 2, -2, 3, -3, 4)
NT = (((1,), (1,)), ((), ()))
NN = (((1,), (0,)), ((), ()))


def kernel(
    mask_s, order_v, q_h, k_h, v_h, w_h, dy_h,
    mixed_o, gq_o, gk_o, gv_o, gw_o,
    q_v, dy2, kb, vb, order_n, w_full,
    qst, dast, ktr, vtr, st, pf, pb, dsb, att_t, lhs, att,
    part_k, part_v, got_k, got_v,
    ga, gb, ra1, rb1, ga2, gb2, ra2, rb2, gy, ry,
    loc_sem, halo_ss, halo_rs, wz_ss, wz_rs, wx_ss, wx_rs, wc_ss, wc_rs,
    core_ss, core_rs, ph_ss, ph_rs,
    a1_ss, a1_rs, b1_ss, b1_rs, a2_ss, a2_rs, b2_ss, b2_rs, y_ss, y_rs,
):
    c = lax.axis_index("ctx")
    d = lax.axis_index("dp")
    xh, y = c // 8, c % 8
    z, xl, k = d // 8, (d // 2) % 4, d % 2
    x = xh * 4 + xl

    def dev(x_, y_, z_, k_):
        return ((x_ // 4) * 8 + y_, z_ * 8 + (x_ % 4) * 2 + k_)

    def zdev(s):
        return dev(x, y, (z + s + 8) % 8, k)

    def xdev(s):
        return dev((x + s + 8) % 8, y, z, k)

    def ydev(s):
        return dev(x, (y + s + 8) % 8, z, k)

    def cdev(s):
        return ((c + s + 16) % 16, d)

    other = 1 - k
    mate = dev(x, y, z, other)

    def rcopy(src, dst, ss, rs, to):
        return pltpu.make_async_remote_copy(
            src_ref=src, dst_ref=dst, send_sem=ss, recv_sem=rs, device_id=to, device_id_type=MESH
        )

    loc = [
        pltpu.make_async_copy(q_h, q_v, loc_sem.at[0]),
        pltpu.make_async_copy(k_h, kb.at[1], loc_sem.at[1]),
        pltpu.make_async_copy(v_h, vb.at[1], loc_sem.at[2]),
        pltpu.make_async_copy(dy_h, dy2.at[0], loc_sem.at[3]),
        pltpu.make_async_copy(w_h, w_full.at[z, xl, k], loc_sem.at[4]),
    ]
    for cp in loc:
        cp.start()

    bar = pltpu.get_barrier_semaphore()
    friends = [cdev(1), cdev(-1), mate]
    for s in D7:
        friends += [zdev(s), xdev(s), ydev(s)]
    for f in friends:
        pl.semaphore_signal(bar, inc=1, device_id=f, device_id_type=MESH)
    pl.semaphore_wait(bar, len(friends))

    sends = []

    def go(cp):
        cp.start()
        sends.append(cp)
        return cp

    halo = []
    for i, (s, slot) in enumerate(((1, 0), (-1, 2))):
        halo.append(go(rcopy(k_h, kb.at[slot], halo_ss.at[3 * i], halo_rs.at[3 * i], cdev(s))))
        halo.append(go(rcopy(v_h, vb.at[slot], halo_ss.at[3 * i + 1], halo_rs.at[3 * i + 1], cdev(s))))
        halo.append(go(rcopy(order_v, order_n.at[i], halo_ss.at[3 * i + 2], halo_rs.at[3 * i + 2], cdev(s))))
    for i, s in enumerate(D7):
        go(rcopy(w_h, w_full.at[z, xl, k], wz_ss.at[i], wz_rs.at[i], zdev(s)))
    dy_c = go(rcopy(dy_h, dy2.at[1], core_ss.at[0], core_rs.at[0], mate))

    for cp in loc[:3]:
        cp.wait()
    for h in range(8):
        qst[h * T : (h + 1) * T, :] = q_v[:, h * HD : (h + 1) * HD]
    for g in range(GROUPS):
        st[g, T : 2 * T, :] = lax.dot_general(
            kb[1, :, g * HD : (g + 1) * HD], qst[g * 512 : (g + 1) * 512, :], NT,
            preferred_element_type=F32,
        )
    jcol = lax.broadcasted_iota(jnp.int32, (T, T), 1)
    irow = lax.broadcasted_iota(jnp.int32, (T, T), 0)
    jblk = jcol // BLK

    def key_block(order):
        hit = irow == jnp.broadcast_to(order, (T, T))
        return jnp.sum(jnp.where(hit, jblk, 0).astype(F32), axis=1, keepdims=True)

    own_hit = (irow == jnp.broadcast_to(order_v[...], (T, T))).astype(F32).astype(BF)
    jrow = (lax.broadcasted_iota(jnp.int32, (8, T), 1) // BLK).astype(F32).astype(BF)
    q_block = lax.dot_general(jrow, own_hit, NT, preferred_element_type=F32)[0:1]

    loc[4].wait()
    for i, s in enumerate(D7):
        there = w_full.at[(z - s + 8) % 8, xl, k]
        rcopy(w_h, there, wz_ss.at[i], wz_rs.at[i], zdev(s)).wait_recv()
    column = w_full.at[:, xl, k]
    go(rcopy(column, column, wx_ss.at[0], wx_rs.at[0], xdev(1)))
    go(rcopy(column, column, wx_ss.at[1], wx_rs.at[1], xdev(-1)))
    for i, s in ((2, 2), (3, -2)):
        part = w_full.at[pl.ds((i - 2) * 4, 4), xl, k]
        go(rcopy(part, part, wx_ss.at[i], wx_rs.at[i], xdev(s)))
    go(rcopy(column, column, wc_ss.at[0], wc_rs.at[0], mate))

    for cp in halo:
        cp.wait_recv()
    for i, slot in ((0, 0), (1, 2)):
        kblk = key_block(order_n[i])
        allow = jnp.zeros((T, T), F32)
        for b2 in range(4):
            row = jnp.zeros((1, T), F32)
            for b1 in range(4):
                seen = jnp.full((1, T), mask_s[b1, 4 * i + b2], jnp.int32).astype(F32)
                row = row + jnp.where(q_block == float(b1), seen, 0.0)
            allow = allow + jnp.where(kblk == float(b2), jnp.broadcast_to(row, (T, T)), 0.0)
        allow4 = jnp.concatenate([allow] * GROUP, axis=1)
        for g in range(GROUPS):
            s_g = lax.dot_general(
                kb[slot, :, g * HD : (g + 1) * HD], qst[g * 512 : (g + 1) * 512, :], NT,
                preferred_element_type=F32,
            )
            st[g, slot * T : (slot + 1) * T, :] = jnp.where(allow4 > 0.5, s_g, -1e30)
    scale = 1.0 / math.sqrt(HD)
    to_two = scale * math.log2(math.e)
    for g in range(GROUPS):
        top = jnp.max(st[g], axis=0, keepdims=True)
        e = jnp.exp2((st[g] - top) * to_two)
        p = e * (1.0 / jnp.sum(e, axis=0, keepdims=True))
        pf[g] = p
        pb[g] = p.astype(BF)
        v_g = vb[:, :, g * HD : (g + 1) * HD].reshape(3 * T, HD)
        vtr[g] = v_g.T
        at = jnp.dot(vtr[g], pb[g], preferred_element_type=F32).astype(BF)
        for j in range(GROUP):
            h = g * GROUP + j
            att_t[h * 4 : (h + 1) * 4] = at[:, j * T : (j + 1) * T].reshape(4, 2, 16, T)
            att[:, h * HD : (h + 1) * HD] = at[:, j * T : (j + 1) * T].T
    a_c = go(rcopy(att_t.at[:, other], lhs.at[1], core_ss.at[1], core_rs.at[1], mate))
    for g in range(GROUPS):
        ktr[g] = kb[:, :, g * HD : (g + 1) * HD].reshape(3 * T, HD).T

    loc[3].wait()
    dy_c.wait_recv()
    lhs[0] = att_t[:, k]
    a_c.wait_recv()
    left = jnp.concatenate([lhs[0].reshape(512, T), lhs[1].reshape(512, T)], axis=1)
    right = dy2[...].reshape(2 * T, D)
    for xh_ in range(2):
        g_a = jnp.dot(left, right[:, xh_ * 512 : xh_ * 512 + 256], preferred_element_type=F32)
        ga[:, :, :, xh_ * 256 : (xh_ + 1) * 256] = g_a.astype(BF).reshape(8, 4, 16, 256)
    a1 = []
    for i, s in enumerate(D7):
        a1.append(go(rcopy(ga.at[(z + s + 8) % 8], ra1.at[i], a1_ss.at[i], a1_rs.at[i], zdev(s))))
    for xh_ in range(2):
        g_b = jnp.dot(left, right[:, xh_ * 512 + 256 : xh_ * 512 + 512], preferred_element_type=F32)
        g_b = g_b.astype(BF).reshape(8, 4, 16, 256)
        for xl_ in range(4):
            gb[xh_ * 4 + xl_] = g_b[:, xl_]
    b1 = []
    for i, s in enumerate(D7):
        b1.append(go(rcopy(gb.at[(x + s + 8) % 8], rb1.at[i], b1_ss.at[i], b1_rs.at[i], xdev(s))))

    for i, s in ((0, 1), (1, -1)):
        there = w_full.at[:, (xl - s + 4) % 4, k]
        rcopy(there, there, wx_ss.at[i], wx_rs.at[i], xdev(s)).wait_recv()
        go(rcopy(there, there, wc_ss.at[i + 1], wc_rs.at[i + 1], mate))
    for i, s in ((2, 2), (3, -2)):
        there = w_full.at[pl.ds((i - 2) * 4, 4), (xl + 2) % 4, k]
        rcopy(there, there, wx_ss.at[i], wx_rs.at[i], xdev(s)).wait_recv()
    there = w_full.at[:, (xl + 2) % 4, k]
    go(rcopy(there, there, wc_ss.at[3], wc_rs.at[3], mate))
    for i, s in ((0, 0), (1, -1), (2, 1), (3, 2)):
        there = w_full.at[:, (xl + s + 4) % 4, other]
        rcopy(there, there, wc_ss.at[i], wc_rs.at[i], mate).wait_recv()

    for h in range(8):
        dast[h * T : (h + 1) * T, :] = lax.dot_general(
            dy2[0], w_full[h].reshape(HD, D), NT, preferred_element_type=F32
        ).astype(BF)
    part = []
    for g in range(GROUPS):
        pv = jnp.dot(pb[g], dast[g * 512 : (g + 1) * 512, :], preferred_element_type=F32)
        part_v[:, :, g * HD : (g + 1) * HD] = pv.astype(BF).reshape(3, T, HD)
    part.append(go(rcopy(part_v.at[0], got_v.at[0], ph_ss.at[0], ph_rs.at[0], cdev(-1))))
    part.append(go(rcopy(part_v.at[2], got_v.at[1], ph_ss.at[1], ph_rs.at[1], cdev(1))))
    for g in range(GROUPS):
        v_g = vb[:, :, g * HD : (g + 1) * HD].reshape(3 * T, HD)
        dp_ = lax.dot_general(
            v_g, dast[g * 512 : (g + 1) * 512, :], NT, preferred_element_type=F32
        )
        delta = jnp.sum(pb[g].astype(F32) * dp_, axis=0, keepdims=True)
        dsb[g] = (pf[g] * (dp_ - delta)).astype(BF)
        pk = jnp.dot(dsb[g], qst[g * 512 : (g + 1) * 512, :], preferred_element_type=F32)
        part_k[:, :, g * HD : (g + 1) * HD] = (pk * scale).astype(BF).reshape(3, T, HD)
    part.append(go(rcopy(part_k.at[0], got_k.at[0], ph_ss.at[2], ph_rs.at[2], cdev(-1))))
    part.append(go(rcopy(part_k.at[2], got_k.at[1], ph_ss.at[3], ph_rs.at[3], cdev(1))))

    for cp in a1:
        cp.wait_recv()
    s_a = ga[z].astype(F32)
    for i in range(7):
        s_a = s_a + ra1[i].astype(F32)
    s_a = s_a.astype(BF)
    for xh_ in range(2):
        ga2[xh_ * 4 : (xh_ + 1) * 4] = s_a[:, :, xh_ * 256 : (xh_ + 1) * 256]
    a2 = []
    for i, s in enumerate(D7):
        a2.append(go(rcopy(ga2.at[(x + s + 8) % 8], ra2.at[i], a2_ss.at[i], a2_rs.at[i], xdev(s))))
    for cp in b1:
        cp.wait_recv()
    s_b = gb[x].astype(F32)
    for i in range(7):
        s_b = s_b + rb1[i].astype(F32)
    gb2[...] = s_b.astype(BF)
    b2 = []
    for i, s in enumerate(D7):
        b2.append(go(rcopy(gb2.at[(z + s + 8) % 8], rb2.at[i], b2_ss.at[i], b2_rs.at[i], zdev(s))))

    mixed_o[...] = jnp.dot(
        att[...], w_full[...].reshape(D, D), preferred_element_type=F32
    ).astype(BF)
    for g in range(GROUPS):
        gq = jnp.dot(ktr[g], dsb[g], preferred_element_type=F32) * scale
        for j in range(GROUP):
            h = g * GROUP + j
            gq_o[:, h * HD : (h + 1) * HD] = gq[:, j * T : (j + 1) * T].astype(BF).T

    for cp in a2:
        cp.wait_recv()
    f_a = ga2[x].astype(F32)
    for i in range(7):
        f_a = f_a + ra2[i].astype(F32)
    gy[0] = f_a[:, :128]
    gy[1] = f_a[:, 128:]
    for cp in b2:
        cp.wait_recv()
    f_b = gb2[z].astype(F32)
    for i in range(7):
        f_b = f_b + rb2[i].astype(F32)
    gy[2] = f_b[:, :128]
    gy[3] = f_b[:, 128:]
    legs = []
    for i, s in enumerate(D7):
        to = (y + s + 8) % 8
        legs.append(go(rcopy(gy.at[to // 2], ry.at[i], y_ss.at[i], y_rs.at[i], ydev(s))))

    for cp in part:
        cp.wait_recv()
    gv_o[...] = (part_v[1].astype(F32) + got_v[0].astype(F32) + got_v[1].astype(F32)).astype(BF)
    gk_o[...] = (part_k[1].astype(F32) + got_k[0].astype(F32) + got_k[1].astype(F32)).astype(BF)

    for cp in legs:
        cp.wait_recv()
    total = gy[y // 2]
    for i in range(7):
        total = total + ry[i]
    norm = 1.0 / math.sqrt(64 * 16 * T)
    odd = jnp.full((16, 64), y % 2, jnp.int32) > 0
    gw_o[...] = jnp.where(odd, total[:, 64:], total[:, :64]) * norm

    for cp in sends:
        cp.wait_send()


def shards(queries, keys_in, values_in, patch_order, block_mask, out_weight, cotangent):
    dma = pltpu.SemaphoreType.DMA
    vm = pltpu.VMEM
    any_ = pl.BlockSpec(memory_space=pl.ANY)
    in_vmem = pl.BlockSpec(memory_space=pltpu.VMEM)
    scratch = [
        vm((T, D), BF),
        vm((2, T, D), BF),
        vm((3, T, KV), BF),
        vm((3, T, KV), BF),
        vm((2, 1, T), jnp.int32),
        vm((8, 4, 2, 16, D), BF),
        vm((8 * T, HD), BF),
        vm((8 * T, HD), BF),
        vm((GROUPS, HD, 3 * T), BF),
        vm((GROUPS, HD, 3 * T), BF),
        vm((GROUPS, 3 * T, 512), F32),
        vm((GROUPS, 3 * T, 512), F32),
        vm((GROUPS, 3 * T, 512), BF),
        vm((GROUPS, 3 * T, 512), BF),
        vm((32, 2, 16, T), BF),
        vm((2, 32, 16, T), BF),
        vm((T, D), BF),
        vm((3, T, KV), BF),
        vm((3, T, KV), BF),
        vm((2, T, KV), BF),
        vm((2, T, KV), BF),
        vm((8, 4, 16, 512), BF),
        vm((8, 8, 16, 256), BF),
        vm((7, 4, 16, 512), BF),
        vm((7, 8, 16, 256), BF),
        vm((8, 16, 256), BF),
        vm((8, 16, 256), BF),
        vm((7, 16, 256), BF),
        vm((7, 16, 256), BF),
        vm((4, 16, 128), F32),
        vm((7, 16, 128), F32),
        dma((5,)),
        dma((6,)), dma((6,)),
        dma((7,)), dma((7,)),
        dma((4,)), dma((4,)),
        dma((4,)), dma((4,)),
        dma((2,)), dma((2,)),
        dma((4,)), dma((4,)),
        dma((7,)), dma((7,)),
        dma((7,)), dma((7,)),
        dma((7,)), dma((7,)),
        dma((7,)), dma((7,)),
        dma((7,)), dma((7,)),
    ]
    out = pl.pallas_call(
        kernel,
        out_shape=(
            jax.ShapeDtypeStruct((T, D), BF),
            jax.ShapeDtypeStruct((T, D), BF),
            jax.ShapeDtypeStruct((T, KV), BF),
            jax.ShapeDtypeStruct((T, KV), BF),
            jax.ShapeDtypeStruct((16, 64), F32),
        ),
        in_specs=[pl.BlockSpec(memory_space=pltpu.SMEM), in_vmem, any_, any_, any_, any_, any_],
        out_specs=(in_vmem,) * 5,
        scratch_shapes=scratch,
        compiler_params=pltpu.CompilerParams(
            collective_id=0, has_side_effects=True, vmem_limit_bytes=40 << 20
        ),
        cost_estimate=pl.CostEstimate(
            flops=1_400_000_000, bytes_accessed=1_500_000, transcendentals=400_000
        ),
        name="sublayer",
    )(
        block_mask[0], patch_order[0], queries[0], keys_in[0], values_in[0], out_weight, cotangent[0]
    )
    mixed, gq, gk, gv, gw = out
    return mixed[None], gq[None], gk[None], gv[None], gw


def solution(mesh):
    tokens = P("dp", "ctx", None)
    in_specs = (tokens, tokens, tokens, tokens, tokens, P("dp", None), tokens)
    out_specs = (tokens, tokens, tokens, tokens, P("dp", "ctx"))
    return jax.shard_map(shards, mesh=mesh, in_specs=in_specs, out_specs=out_specs, check_vma=False)
```

```python
import functools
import math

import jax
import jax.numpy as jnp
from jax import lax
from jax.experimental import pallas as pl
from jax.experimental.pallas import tpu as pltpu
from jax.sharding import PartitionSpec as P

MESH = pl.DeviceIdType.MESH
BF = jnp.bfloat16
F32 = jnp.float32
HD = 128
T = 128
D = 1024
GROUP = 4
GROUPS = 2
KV = 256
BLK = 32
VMEM_LIMIT = 60 << 20
D7 = (1, -1, 2, -2, 3, -3, 4)
NT = (((1,), (1,)), ((), ()))
NN = (((1,), (0,)), ((), ()))


def kernel(
    order_h, mask_h, q_h, k_h, v_h, w_h, dy_h,
    mixed_o, gq_o, gk_o, gv_o, gw_o,
    mask_s, order_v, q_v, dy2, kb, vb, order_n, w_full,
    qst, dast, ktr, vtr, st, pf, pb, dsb, att_t, lhs, att,
    part_k, part_v, got_k, got_v,
    dyp, ga, gc, ra1, rc1, ga2, gc2, ra2, rc2, gx, rx,
    loc_sem, halo_ss, halo_rs, wz_ss, wz_rs, wx_ss, wx_rs, wc_ss, wc_rs,
    core_ss, core_rs, ph_ss, ph_rs,
    a1_ss, a1_rs, c1_ss, c1_rs, a2_ss, a2_rs, c2_ss, c2_rs, x_ss, x_rs,
):
    c = lax.axis_index("ctx")
    d = lax.axis_index("dp")
    xh, y = c // 8, c % 8
    z, xl, k = d // 8, (d // 2) % 4, d % 2
    x = xh * 4 + xl

    def dev(x_, y_, z_, k_):
        return ((x_ // 4) * 8 + y_, z_ * 8 + (x_ % 4) * 2 + k_)

    def zdev(s):
        return dev(x, y, (z + s + 8) % 8, k)

    def xdev(s):
        return dev((x + s + 8) % 8, y, z, k)

    def ydev(s):
        return dev(x, (y + s + 8) % 8, z, k)

    def cdev(s):
        return ((c + s + 16) % 16, d)

    other = 1 - k
    mate = dev(x, y, z, other)

    def rcopy(src, dst, ss, rs, to):
        return pltpu.make_async_remote_copy(
            src_ref=src, dst_ref=dst, send_sem=ss, recv_sem=rs, device_id=to, device_id_type=MESH
        )

    loc = [
        pltpu.make_async_copy(q_h, q_v, loc_sem.at[0]),
        pltpu.make_async_copy(k_h, kb.at[1], loc_sem.at[1]),
        pltpu.make_async_copy(v_h, vb.at[1], loc_sem.at[2]),
        pltpu.make_async_copy(dy_h, dy2.at[0], loc_sem.at[3]),
        pltpu.make_async_copy(w_h, w_full.at[z, xl, k], loc_sem.at[4]),
        pltpu.make_async_copy(order_h, order_v, loc_sem.at[5]),
        pltpu.make_async_copy(mask_h, mask_s, loc_sem.at[6]),
    ]
    for cp in loc:
        cp.start()

    bar = pltpu.get_barrier_semaphore()
    friends = [cdev(1), cdev(-1), mate]
    for s in D7:
        friends += [zdev(s), xdev(s), ydev(s)]
    for f in friends:
        pl.semaphore_signal(bar, inc=1, device_id=f, device_id_type=MESH)
    loc[5].wait()
    loc[6].wait()
    pl.semaphore_wait(bar, len(friends))

    sends = []

    def go(cp):
        cp.start()
        sends.append(cp)
        return cp

    halo = []
    for i, (s, slot) in enumerate(((1, 0), (-1, 2))):
        halo.append(go(rcopy(k_h, kb.at[slot], halo_ss.at[3 * i], halo_rs.at[3 * i], cdev(s))))
        halo.append(go(rcopy(v_h, vb.at[slot], halo_ss.at[3 * i + 1], halo_rs.at[3 * i + 1], cdev(s))))
        halo.append(go(rcopy(order_h, order_n.at[i], halo_ss.at[3 * i + 2], halo_rs.at[3 * i + 2], cdev(s))))
    for i, s in enumerate(D7):
        go(rcopy(w_h, w_full.at[z, xl, k], wz_ss.at[i], wz_rs.at[i], zdev(s)))
    xs = [(1, -1, 2 if j % 2 else -2) for j in range(8)]

    def pass_on(src, j, place):
        for m, s in enumerate(xs[j]):
            go(rcopy(src, place, wx_ss.at[3 * j + m], wx_rs.at[3 * j + m], xdev(s)))
        go(rcopy(src, place, wc_ss.at[j], wc_rs.at[0], mate))

    pass_on(w_h, 0, w_full.at[z, xl, k])
    dy_c = go(rcopy(dy_h, dy2.at[1], core_ss.at[0], core_rs.at[0], mate))

    for cp in loc[:3]:
        cp.wait()
    for h in range(8):
        qst[h * T : (h + 1) * T, :] = q_v[:, h * HD : (h + 1) * HD]
    for g in range(GROUPS):
        st[g, T : 2 * T, :] = lax.dot_general(
            kb[1, :, g * HD : (g + 1) * HD], qst[g * 512 : (g + 1) * 512, :], NT,
            preferred_element_type=F32,
        )
    jcol = lax.broadcasted_iota(jnp.int32, (T, T), 1)
    irow = lax.broadcasted_iota(jnp.int32, (T, T), 0)
    jblk = jcol // BLK

    def key_block(order):
        hit = irow == jnp.broadcast_to(order, (T, T))
        return jnp.sum(jnp.where(hit, jblk, 0).astype(F32), axis=1, keepdims=True)

    own_hit = (irow == jnp.broadcast_to(order_v[...], (T, T))).astype(F32).astype(BF)
    jrow = (lax.broadcasted_iota(jnp.int32, (8, T), 1) // BLK).astype(F32).astype(BF)
    q_block = lax.dot_general(jrow, own_hit, NT, preferred_element_type=F32)[0:1]

    for i, s in enumerate(D7):
        there = w_full.at[(z - s + 8) % 8, xl, k]
        rcopy(w_h, there, wz_ss.at[i], wz_rs.at[i], zdev(s)).wait_recv()
        pass_on(there, i + 1, there)

    def order_columns(i):
        for y_ in range(8):
            lo = dy2[i, :, y_ * 64 : y_ * 64 + 64]
            hi = dy2[i, :, 512 + y_ * 64 : 576 + y_ * 64]
            dyp[i * T : (i + 1) * T, y_ * 128 : (y_ + 1) * 128] = jnp.concatenate([lo, hi], axis=1)

    loc[3].wait()
    order_columns(0)

    for cp in halo:
        cp.wait_recv()
    for i, slot in ((0, 0), (1, 2)):
        kblk = key_block(order_n[i])
        allow = jnp.zeros((T, T), F32)
        for b2 in range(4):
            row = jnp.zeros((1, T), F32)
            for b1 in range(4):
                seen = jnp.full((1, T), mask_s[b1, 4 * i + b2], jnp.int32).astype(F32)
                row = row + jnp.where(q_block == float(b1), seen, 0.0)
            allow = allow + jnp.where(kblk == float(b2), jnp.broadcast_to(row, (T, T)), 0.0)
        allow4 = jnp.concatenate([allow] * GROUP, axis=1)
        for g in range(GROUPS):
            s_g = lax.dot_general(
                kb[slot, :, g * HD : (g + 1) * HD], qst[g * 512 : (g + 1) * 512, :], NT,
                preferred_element_type=F32,
            )
            st[g, slot * T : (slot + 1) * T, :] = jnp.where(allow4 > 0.5, s_g, -1e30)
    scale = 1.0 / math.sqrt(HD)
    to_two = scale * math.log2(math.e)
    for g in range(GROUPS):
        top = jnp.max(st[g], axis=0, keepdims=True)
        e = jnp.exp2((st[g] - top) * to_two)
        p = e * (1.0 / jnp.sum(e, axis=0, keepdims=True))
        pf[g] = p
        pb[g] = p.astype(BF)
        v_g = vb[:, :, g * HD : (g + 1) * HD].reshape(3 * T, HD)
        vtr[g] = v_g.T
        at = jnp.dot(vtr[g], pb[g], preferred_element_type=F32).astype(BF)
        for j in range(GROUP):
            h = g * GROUP + j
            att_t[h * 4 : (h + 1) * 4] = at[:, j * T : (j + 1) * T].reshape(4, 2, 16, T)
            att[:, h * HD : (h + 1) * HD] = at[:, j * T : (j + 1) * T].T
    a_c = go(rcopy(att_t.at[:, other], lhs.at[1], core_ss.at[1], core_rs.at[1], mate))
    for g in range(GROUPS):
        ktr[g] = kb[:, :, g * HD : (g + 1) * HD].reshape(3 * T, HD).T

    dy_c.wait_recv()
    order_columns(1)
    lhs[0] = att_t[:, k]
    a_c.wait_recv()
    left = jnp.concatenate([lhs[0], lhs[1]], axis=2).reshape(8, 4, 16, 2 * T)
    g_a = jnp.dot(left[:, :2].reshape(256, 2 * T), dyp[...], preferred_element_type=F32)
    ga[...] = g_a.astype(BF).reshape(8, 2, 16, D)
    a1 = []
    for i, s in enumerate(D7):
        a1.append(go(rcopy(ga.at[(z + s + 8) % 8], ra1.at[i], a1_ss.at[i], a1_rs.at[i], zdev(s))))
    g_c = jnp.dot(left[:, 2:].reshape(256, 2 * T), dyp[...], preferred_element_type=F32)
    for y_ in range(8):
        gc[y_] = g_c[:, y_ * 128 : (y_ + 1) * 128].astype(BF).reshape(8, 2, 16, 128)
    c1 = []
    for i, s in enumerate(D7):
        c1.append(go(rcopy(gc.at[(y + s + 8) % 8], rc1.at[i], c1_ss.at[i], c1_rs.at[i], ydev(s))))

    for j in range(8):
        zj = z if j == 0 else (z - D7[j - 1] + 8) % 8
        for m, s in enumerate(xs[j]):
            there = w_full.at[zj, (xl - s + 4) % 4, k]
            rcopy(there, there, wx_ss.at[3 * j + m], wx_rs.at[3 * j + m], xdev(s)).wait_recv()
            go(rcopy(there, there, wc_ss.at[8 + 3 * j + m], wc_rs.at[0], mate))
    loc[4].wait()
    there = w_full.at[:, :, other]
    rcopy(there, there, wc_ss.at[0], wc_rs.at[0], mate).wait_recv()
    for h in range(8):
        dast[h * T : (h + 1) * T, :] = lax.dot_general(
            dy2[0], w_full[h].reshape(HD, D), NT, preferred_element_type=F32
        ).astype(BF)
    part = []
    for g in range(GROUPS):
        pv = jnp.dot(pb[g], dast[g * 512 : (g + 1) * 512, :], preferred_element_type=F32)
        part_v[:, :, g * HD : (g + 1) * HD] = pv.astype(BF).reshape(3, T, HD)
    part.append(go(rcopy(part_v.at[0], got_v.at[0], ph_ss.at[0], ph_rs.at[0], cdev(-1))))
    part.append(go(rcopy(part_v.at[2], got_v.at[1], ph_ss.at[1], ph_rs.at[1], cdev(1))))
    for g in range(GROUPS):
        v_g = vb[:, :, g * HD : (g + 1) * HD].reshape(3 * T, HD)
        dp_ = lax.dot_general(
            v_g, dast[g * 512 : (g + 1) * 512, :], NT, preferred_element_type=F32
        )
        delta = jnp.sum(pb[g].astype(F32) * dp_, axis=0, keepdims=True)
        dsb[g] = (pf[g] * (dp_ - delta)).astype(BF)
        pk = jnp.dot(dsb[g], qst[g * 512 : (g + 1) * 512, :], preferred_element_type=F32)
        part_k[:, :, g * HD : (g + 1) * HD] = (pk * scale).astype(BF).reshape(3, T, HD)
    part.append(go(rcopy(part_k.at[0], got_k.at[0], ph_ss.at[2], ph_rs.at[2], cdev(-1))))
    part.append(go(rcopy(part_k.at[2], got_k.at[1], ph_ss.at[3], ph_rs.at[3], cdev(1))))

    for cp in a1:
        cp.wait_recv()
    s_a = ga[z].astype(F32)
    for i in range(7):
        s_a = s_a + ra1[i].astype(F32)
    s_a = s_a.astype(BF)
    for y_ in range(8):
        ga2[y_] = s_a[:, :, y_ * 128 : (y_ + 1) * 128]
    a2 = []
    for i, s in enumerate(D7):
        a2.append(go(rcopy(ga2.at[(y + s + 8) % 8], ra2.at[i], a2_ss.at[i], a2_rs.at[i], ydev(s))))
    for cp in c1:
        cp.wait_recv()
    s_c = gc[y].astype(F32)
    for i in range(7):
        s_c = s_c + rc1[i].astype(F32)
    gc2[...] = s_c.astype(BF)
    c2 = []
    for i, s in enumerate(D7):
        c2.append(go(rcopy(gc2.at[(z + s + 8) % 8], rc2.at[i], c2_ss.at[i], c2_rs.at[i], zdev(s))))

    mixed_o[...] = jnp.dot(
        att[...], w_full[...].reshape(D, D), preferred_element_type=F32
    ).astype(BF)
    for g in range(GROUPS):
        gq = jnp.dot(ktr[g], dsb[g], preferred_element_type=F32) * scale
        for j in range(GROUP):
            h = g * GROUP + j
            gq_o[:, h * HD : (h + 1) * HD] = gq[:, j * T : (j + 1) * T].astype(BF).T

    for cp in a2:
        cp.wait_recv()
    f_a = ga2[y].astype(F32)
    for i in range(7):
        f_a = f_a + ra2[i].astype(F32)
    gx[0:2] = f_a
    for cp in c2:
        cp.wait_recv()
    f_c = gc2[z].astype(F32)
    for i in range(7):
        f_c = f_c + rc2[i].astype(F32)
    gx[2:4] = f_c
    legs = []
    for i, s in enumerate(D7):
        to = (xl + s + 8) % 4
        legs.append(go(rcopy(gx.at[to], rx.at[i], x_ss.at[i], x_rs.at[i], xdev(s))))

    for cp in part:
        cp.wait_recv()
    gv_o[...] = (part_v[1].astype(F32) + got_v[0].astype(F32) + got_v[1].astype(F32)).astype(BF)
    gk_o[...] = (part_k[1].astype(F32) + got_k[0].astype(F32) + got_k[1].astype(F32)).astype(BF)

    for cp in legs:
        cp.wait_recv()
    total = gx[xl]
    for i in range(7):
        total = total + rx[i]
    norm = 1.0 / math.sqrt(64 * 16 * T)
    high = jnp.full((16, 64), xh, jnp.int32) > 0
    gw_o[...] = jnp.where(high, total[:, 64:], total[:, :64]) * norm

    for cp in sends:
        cp.wait_send()


def store(*refs):
    ins, outs, room, sem = refs[:5], refs[5:10], refs[10:15], refs[15]
    loads = [pltpu.make_async_copy(ins[i], room[i], sem.at[i]) for i in range(5)]
    saves = [pltpu.make_async_copy(room[i], outs[i], sem.at[5 + i]) for i in range(5)]
    for cp in loads:
        cp.start()
    for load, save in zip(loads, saves):
        load.wait()
        save.start()
    for cp in saves:
        cp.wait()


def shards(queries, keys_in, values_in, patch_order, block_mask, out_weight, cotangent):
    dma = pltpu.SemaphoreType.DMA
    vm = pltpu.VMEM
    hbm = pl.BlockSpec(memory_space=pltpu.HBM)
    in_vmem = pl.BlockSpec(memory_space=pltpu.VMEM)
    scratch = [
        pltpu.SMEM((4, 8), jnp.int32),
        vm((1, T), jnp.int32),
        vm((T, D), BF),
        vm((2, T, D), BF),
        vm((3, T, KV), BF),
        vm((3, T, KV), BF),
        vm((2, 1, T), jnp.int32),
        vm((8, 4, 2, 16, D), BF),
        vm((8 * T, HD), BF),
        vm((8 * T, HD), BF),
        vm((GROUPS, HD, 3 * T), BF),
        vm((GROUPS, HD, 3 * T), BF),
        vm((GROUPS, 3 * T, 512), F32),
        vm((GROUPS, 3 * T, 512), F32),
        vm((GROUPS, 3 * T, 512), BF),
        vm((GROUPS, 3 * T, 512), BF),
        vm((32, 2, 16, T), BF),
        vm((2, 32, 16, T), BF),
        vm((T, D), BF),
        vm((3, T, KV), BF),
        vm((3, T, KV), BF),
        vm((2, T, KV), BF),
        vm((2, T, KV), BF),
        vm((2 * T, D), BF),
        vm((8, 2, 16, D), BF),
        vm((8, 8, 2, 16, 128), BF),
        vm((7, 2, 16, D), BF),
        vm((7, 8, 2, 16, 128), BF),
        vm((8, 2, 16, 128), BF),
        vm((8, 2, 16, 128), BF),
        vm((7, 2, 16, 128), BF),
        vm((7, 2, 16, 128), BF),
        vm((4, 16, 128), F32),
        vm((7, 16, 128), F32),
        dma((7,)),
        dma((6,)), dma((6,)),
        dma((7,)), dma((7,)),
        dma((24,)), dma((24,)),
        dma((32,)), dma((1,)),
        dma((2,)), dma((2,)),
        dma((4,)), dma((4,)),
        dma((7,)), dma((7,)),
        dma((7,)), dma((7,)),
        dma((7,)), dma((7,)),
        dma((7,)), dma((7,)),
        dma((7,)), dma((7,)),
    ]
    out = pl.pallas_call(
        kernel,
        out_shape=(
            jax.ShapeDtypeStruct((T, D), BF),
            jax.ShapeDtypeStruct((T, D), BF),
            jax.ShapeDtypeStruct((T, KV), BF),
            jax.ShapeDtypeStruct((T, KV), BF),
            jax.ShapeDtypeStruct((16, 64), F32),
        ),
        in_specs=[hbm] * 7,
        out_specs=(in_vmem,) * 5,
        scratch_shapes=scratch,
        compiler_params=pltpu.CompilerParams(
            collective_id=0, has_side_effects=True, vmem_limit_bytes=VMEM_LIMIT
        ),
        cost_estimate=pl.CostEstimate(
            flops=1_400_000_000, bytes_accessed=1_500_000, transcendentals=400_000
        ),
        name="sublayer",
    )(
        patch_order[0], block_mask[0], queries[0], keys_in[0], values_in[0], out_weight, cotangent[0]
    )
    mixed, gq, gk, gv, gw = pl.pallas_call(
        store,
        out_shape=[jax.ShapeDtypeStruct(o.shape, o.dtype) for o in out],
        in_specs=[hbm] * 5,
        out_specs=[hbm] * 5,
        scratch_shapes=[vm(o.shape, o.dtype) for o in out] + [dma((10,))],
        compiler_params=pltpu.CompilerParams(vmem_limit_bytes=VMEM_LIMIT),
        name="store",
    )(*out)
    return mixed[None], gq[None], gk[None], gv[None], gw


def solution(mesh):
    tokens = P("dp", "ctx", None)
    in_specs = (tokens, tokens, tokens, tokens, tokens, P("dp", None), tokens)
    out_specs = (tokens, tokens, tokens, tokens, P("dp", "ctx"))
    return jax.shard_map(shards, mesh=mesh, in_specs=in_specs, out_specs=out_specs, check_vma=False)
```

```python
import functools
import math

import jax
import jax.numpy as jnp
from jax import lax
from jax.experimental import pallas as pl
from jax.experimental.pallas import tpu as pltpu
from jax.sharding import PartitionSpec as P

MESH = pl.DeviceIdType.MESH
BF = jnp.bfloat16
F32 = jnp.float32
HD = 128
T = 128
D = 1024
GROUP = 4
GROUPS = 2
KV = 256
BLK = 32
VMEM_LIMIT = 60 << 20
D7 = (1, -1, 2, -2, 3, -3, 4)
NT = (((1,), (1,)), ((), ()))
NN = (((1,), (0,)), ((), ()))


def kernel(
    order_h, mask_h, q_h, k_h, v_h, w_h, dy_h,
    mixed_h, gq_h, gk_h, gv_h, gw_h,
    mixed_o, gq_o, gk_o, gv_o, gw_o, out_sem,
    mask_s, order_v, q_v, dy2, kb, vb, order_n, w_full,
    qst, dast, ktr, vtr, st, pf, pb, dsb, att_t, lhs, att,
    part_k, part_v, got_k, got_v,
    dyp, ga, gc, ra1, rc1, ga2, gc2, ra2, rc2, gx, rx,
    loc_sem, halo_ss, halo_rs, wz_ss, wz_rs, wx_ss, wx_rs, wc_ss, wc_rs,
    core_ss, core_rs, ph_ss, ph_rs,
    a1_ss, a1_rs, c1_ss, c1_rs, a2_ss, a2_rs, c2_ss, c2_rs, x_ss, x_rs,
):
    c = lax.axis_index("ctx")
    d = lax.axis_index("dp")
    xh, y = c // 8, c % 8
    z, xl, k = d // 8, (d // 2) % 4, d % 2
    x = xh * 4 + xl

    def dev(x_, y_, z_, k_):
        return ((x_ // 4) * 8 + y_, z_ * 8 + (x_ % 4) * 2 + k_)

    def zdev(s):
        return dev(x, y, (z + s + 8) % 8, k)

    def xdev(s):
        return dev((x + s + 8) % 8, y, z, k)

    def ydev(s):
        return dev(x, (y + s + 8) % 8, z, k)

    def cdev(s):
        return ((c + s + 16) % 16, d)

    other = 1 - k
    mate = dev(x, y, z, other)

    def rcopy(src, dst, ss, rs, to):
        return pltpu.make_async_remote_copy(
            src_ref=src, dst_ref=dst, send_sem=ss, recv_sem=rs, device_id=to, device_id_type=MESH
        )

    loc = [
        pltpu.make_async_copy(q_h, q_v, loc_sem.at[0]),
        pltpu.make_async_copy(k_h, kb.at[1], loc_sem.at[1]),
        pltpu.make_async_copy(v_h, vb.at[1], loc_sem.at[2]),
        pltpu.make_async_copy(dy_h, dy2.at[0], loc_sem.at[3]),
        pltpu.make_async_copy(w_h, w_full.at[z, xl, k], loc_sem.at[4]),
        pltpu.make_async_copy(order_h, order_v, loc_sem.at[5]),
        pltpu.make_async_copy(mask_h, mask_s, loc_sem.at[6]),
    ]
    for cp in loc:
        cp.start()

    bar = pltpu.get_barrier_semaphore()
    friends = [cdev(1), cdev(-1), mate]
    for s in D7:
        friends += [zdev(s), xdev(s), ydev(s)]
    for f in friends:
        pl.semaphore_signal(bar, inc=1, device_id=f, device_id_type=MESH)
    loc[5].wait()
    loc[6].wait()
    pl.semaphore_wait(bar, len(friends))

    sends = []
    saves = []

    def save(i, src, dst):
        cp = pltpu.make_async_copy(src, dst, out_sem.at[i])
        cp.start()
        saves.append(cp)

    def go(cp):
        cp.start()
        sends.append(cp)
        return cp

    halo = []
    for i, (s, slot) in enumerate(((1, 0), (-1, 2))):
        halo.append(go(rcopy(k_h, kb.at[slot], halo_ss.at[3 * i], halo_rs.at[3 * i], cdev(s))))
        halo.append(go(rcopy(v_h, vb.at[slot], halo_ss.at[3 * i + 1], halo_rs.at[3 * i + 1], cdev(s))))
        halo.append(go(rcopy(order_h, order_n.at[i], halo_ss.at[3 * i + 2], halo_rs.at[3 * i + 2], cdev(s))))
    for i, s in enumerate(D7):
        go(rcopy(w_h, w_full.at[z, xl, k], wz_ss.at[i], wz_rs.at[i], zdev(s)))
    dy_c = go(rcopy(dy_h, dy2.at[1], core_ss.at[0], core_rs.at[0], mate))

    for cp in loc[:3]:
        cp.wait()
    for h in range(8):
        qst[h * T : (h + 1) * T, :] = q_v[:, h * HD : (h + 1) * HD]
    for g in range(GROUPS):
        st[g, T : 2 * T, :] = lax.dot_general(
            kb[1, :, g * HD : (g + 1) * HD], qst[g * 512 : (g + 1) * 512, :], NT,
            preferred_element_type=F32,
        )
    jcol = lax.broadcasted_iota(jnp.int32, (T, T), 1)
    irow = lax.broadcasted_iota(jnp.int32, (T, T), 0)
    jblk = jcol // BLK

    def key_block(order):
        hit = irow == jnp.broadcast_to(order, (T, T))
        return jnp.sum(jnp.where(hit, jblk, 0).astype(F32), axis=1, keepdims=True)

    own_hit = (irow == jnp.broadcast_to(order_v[...], (T, T))).astype(F32).astype(BF)
    jrow = (lax.broadcasted_iota(jnp.int32, (8, T), 1) // BLK).astype(F32).astype(BF)
    q_block = lax.dot_general(jrow, own_hit, NT, preferred_element_type=F32)[0:1]

    def order_columns(i):
        for y_ in range(8):
            lo = dy2[i, :, y_ * 64 : y_ * 64 + 64]
            hi = dy2[i, :, 512 + y_ * 64 : 576 + y_ * 64]
            dyp[i * T : (i + 1) * T, y_ * 128 : (y_ + 1) * 128] = jnp.concatenate([lo, hi], axis=1)

    loc[3].wait()
    order_columns(0)

    for cp in halo:
        cp.wait_recv()
    for i, slot in ((0, 0), (1, 2)):
        kblk = key_block(order_n[i])
        allow = jnp.zeros((T, T), F32)
        for b2 in range(4):
            row = jnp.zeros((1, T), F32)
            for b1 in range(4):
                seen = jnp.full((1, T), mask_s[b1, 4 * i + b2], jnp.int32).astype(F32)
                row = row + jnp.where(q_block == float(b1), seen, 0.0)
            allow = allow + jnp.where(kblk == float(b2), jnp.broadcast_to(row, (T, T)), 0.0)
        allow4 = jnp.concatenate([allow] * GROUP, axis=1)
        for g in range(GROUPS):
            s_g = lax.dot_general(
                kb[slot, :, g * HD : (g + 1) * HD], qst[g * 512 : (g + 1) * 512, :], NT,
                preferred_element_type=F32,
            )
            st[g, slot * T : (slot + 1) * T, :] = jnp.where(allow4 > 0.5, s_g, -1e30)
    scale = 1.0 / math.sqrt(HD)
    to_two = scale * math.log2(math.e)
    for g in range(GROUPS):
        top = jnp.max(st[g], axis=0, keepdims=True)
        e = jnp.exp2((st[g] - top) * to_two)
        p = e * (1.0 / jnp.sum(e, axis=0, keepdims=True))
        pf[g] = p
        pb[g] = p.astype(BF)
        v_g = vb[:, :, g * HD : (g + 1) * HD].reshape(3 * T, HD)
        vtr[g] = v_g.T
        at = jnp.dot(vtr[g], pb[g], preferred_element_type=F32).astype(BF)
        for j in range(GROUP):
            h = g * GROUP + j
            att_t[h * 4 : (h + 1) * 4] = at[:, j * T : (j + 1) * T].reshape(4, 2, 16, T)
            att[:, h * HD : (h + 1) * HD] = at[:, j * T : (j + 1) * T].T
    a_c = go(rcopy(att_t.at[:, other], lhs.at[1], core_ss.at[1], core_rs.at[1], mate))
    loc[4].wait()
    for i, s in enumerate(D7):
        there = w_full.at[(z - s + 8) % 8, xl, k]
        rcopy(w_h, there, wz_ss.at[i], wz_rs.at[i], zdev(s)).wait_recv()
    legs_w = ((1, 0), (-1, 0), (2, 0), (1, 1), (-1, 1), (-2, 1))
    for i, (s, half) in enumerate(legs_w):
        rows = w_full.at[pl.ds(half * 4, 4), xl, k]
        go(rcopy(rows, rows, wx_ss.at[i], wx_rs.at[i], xdev(s)))
    column = w_full.at[:, xl, k]
    go(rcopy(column, column, wc_ss.at[0], wc_rs.at[0], mate))
    dy_c.wait_recv()
    order_columns(1)
    lhs[0] = att_t[:, k]
    a_c.wait_recv()
    left = jnp.concatenate([lhs[0], lhs[1]], axis=2).reshape(8, 4, 16, 2 * T)
    g_a = jnp.dot(left[:, :2].reshape(256, 2 * T), dyp[...], preferred_element_type=F32)
    ga[...] = g_a.astype(BF).reshape(8, 2, 16, D)
    a1 = []
    for i, s in enumerate(D7):
        a1.append(go(rcopy(ga.at[(z + s + 8) % 8], ra1.at[i], a1_ss.at[i], a1_rs.at[i], zdev(s))))
    g_c = jnp.dot(left[:, 2:].reshape(256, 2 * T), dyp[...], preferred_element_type=F32)
    for y_ in range(8):
        gc[y_] = g_c[:, y_ * 128 : (y_ + 1) * 128].astype(BF).reshape(8, 2, 16, 128)
    c1 = []
    for i, s in enumerate(D7):
        c1.append(go(rcopy(gc.at[(y + s + 8) % 8], rc1.at[i], c1_ss.at[i], c1_rs.at[i], ydev(s))))

    for g in range(GROUPS):
        ktr[g] = kb[:, :, g * HD : (g + 1) * HD].reshape(3 * T, HD).T
    for i, (s, half) in enumerate(legs_w):
        there = w_full.at[pl.ds(half * 4, 4), (xl - s + 4) % 4, k]
        rcopy(there, there, wx_ss.at[i], wx_rs.at[i], xdev(s)).wait_recv()
        go(rcopy(there, there, wc_ss.at[1 + i], wc_rs.at[0], mate))
    there = w_full.at[:, :, other]
    rcopy(there, there, wc_ss.at[0], wc_rs.at[0], mate).wait_recv()
    for h in range(8):
        dast[h * T : (h + 1) * T, :] = lax.dot_general(
            dy2[0], w_full[h].reshape(HD, D), NT, preferred_element_type=F32
        ).astype(BF)
    part = []
    for g in range(GROUPS):
        pv = jnp.dot(pb[g], dast[g * 512 : (g + 1) * 512, :], preferred_element_type=F32)
        part_v[:, :, g * HD : (g + 1) * HD] = pv.astype(BF).reshape(3, T, HD)
    part.append(go(rcopy(part_v.at[0], got_v.at[0], ph_ss.at[0], ph_rs.at[0], cdev(-1))))
    part.append(go(rcopy(part_v.at[2], got_v.at[1], ph_ss.at[1], ph_rs.at[1], cdev(1))))
    for g in range(GROUPS):
        v_g = vb[:, :, g * HD : (g + 1) * HD].reshape(3 * T, HD)
        dp_ = lax.dot_general(
            v_g, dast[g * 512 : (g + 1) * 512, :], NT, preferred_element_type=F32
        )
        delta = jnp.sum(pb[g].astype(F32) * dp_, axis=0, keepdims=True)
        dsb[g] = (pf[g] * (dp_ - delta)).astype(BF)
        pk = jnp.dot(dsb[g], qst[g * 512 : (g + 1) * 512, :], preferred_element_type=F32)
        part_k[:, :, g * HD : (g + 1) * HD] = (pk * scale).astype(BF).reshape(3, T, HD)
    part.append(go(rcopy(part_k.at[0], got_k.at[0], ph_ss.at[2], ph_rs.at[2], cdev(-1))))
    part.append(go(rcopy(part_k.at[2], got_k.at[1], ph_ss.at[3], ph_rs.at[3], cdev(1))))

    for cp in a1:
        cp.wait_recv()
    s_a = ga[z].astype(F32)
    for i in range(7):
        s_a = s_a + ra1[i].astype(F32)
    s_a = s_a.astype(BF)
    for y_ in range(8):
        ga2[y_] = s_a[:, :, y_ * 128 : (y_ + 1) * 128]
    a2 = []
    for i, s in enumerate(D7):
        a2.append(go(rcopy(ga2.at[(y + s + 8) % 8], ra2.at[i], a2_ss.at[i], a2_rs.at[i], ydev(s))))
    for cp in c1:
        cp.wait_recv()
    s_c = gc[y].astype(F32)
    for i in range(7):
        s_c = s_c + rc1[i].astype(F32)
    gc2[...] = s_c.astype(BF)
    c2 = []
    for i, s in enumerate(D7):
        c2.append(go(rcopy(gc2.at[(z + s + 8) % 8], rc2.at[i], c2_ss.at[i], c2_rs.at[i], zdev(s))))

    mixed_o[...] = jnp.dot(
        att[...], w_full[...].reshape(D, D), preferred_element_type=F32
    ).astype(BF)
    for g in range(GROUPS):
        gq = jnp.dot(ktr[g], dsb[g], preferred_element_type=F32) * scale
        for j in range(GROUP):
            h = g * GROUP + j
            gq_o[:, h * HD : (h + 1) * HD] = gq[:, j * T : (j + 1) * T].astype(BF).T

    save(0, mixed_o, mixed_h)
    save(1, gq_o, gq_h)
    for cp in a2:
        cp.wait_recv()
    f_a = ga2[y].astype(F32)
    for i in range(7):
        f_a = f_a + ra2[i].astype(F32)
    gx[0:2] = f_a
    for cp in c2:
        cp.wait_recv()
    f_c = gc2[z].astype(F32)
    for i in range(7):
        f_c = f_c + rc2[i].astype(F32)
    gx[2:4] = f_c
    legs = []
    for i, s in enumerate(D7):
        to = (xl + s + 8) % 4
        legs.append(go(rcopy(gx.at[to], rx.at[i], x_ss.at[i], x_rs.at[i], xdev(s))))

    for cp in part:
        cp.wait_recv()
    gv_o[...] = (part_v[1].astype(F32) + got_v[0].astype(F32) + got_v[1].astype(F32)).astype(BF)
    gk_o[...] = (part_k[1].astype(F32) + got_k[0].astype(F32) + got_k[1].astype(F32)).astype(BF)

    save(2, gk_o, gk_h)
    save(3, gv_o, gv_h)
    for cp in legs:
        cp.wait_recv()
    total = gx[xl]
    for i in range(7):
        total = total + rx[i]
    norm = 1.0 / math.sqrt(64 * 16 * T)
    high = jnp.full((16, 64), xh, jnp.int32) > 0
    gw_o[...] = jnp.where(high, total[:, 64:], total[:, :64]) * norm

    save(4, gw_o, gw_h)
    for cp in sends:
        cp.wait_send()
    for cp in saves:
        cp.wait()


def store(*refs):
    ins, outs, room, sem = refs[:5], refs[5:10], refs[10:15], refs[15]
    loads = [pltpu.make_async_copy(ins[i], room[i], sem.at[i]) for i in range(5)]
    saves = [pltpu.make_async_copy(room[i], outs[i], sem.at[5 + i]) for i in range(5)]
    for cp in loads:
        cp.start()
    for load, save in zip(loads, saves):
        load.wait()
        save.start()
    for cp in saves:
        cp.wait()


def shards(queries, keys_in, values_in, patch_order, block_mask, out_weight, cotangent):
    dma = pltpu.SemaphoreType.DMA
    vm = pltpu.VMEM
    hbm = pl.BlockSpec(memory_space=pltpu.HBM)
    scratch = [
        vm((T, D), BF),
        vm((T, D), BF),
        vm((T, KV), BF),
        vm((T, KV), BF),
        vm((16, 64), F32),
        dma((5,)),
        pltpu.SMEM((4, 8), jnp.int32),
        vm((1, T), jnp.int32),
        vm((T, D), BF),
        vm((2, T, D), BF),
        vm((3, T, KV), BF),
        vm((3, T, KV), BF),
        vm((2, 1, T), jnp.int32),
        vm((8, 4, 2, 16, D), BF),
        vm((8 * T, HD), BF),
        vm((8 * T, HD), BF),
        vm((GROUPS, HD, 3 * T), BF),
        vm((GROUPS, HD, 3 * T), BF),
        vm((GROUPS, 3 * T, 512), F32),
        vm((GROUPS, 3 * T, 512), F32),
        vm((GROUPS, 3 * T, 512), BF),
        vm((GROUPS, 3 * T, 512), BF),
        vm((32, 2, 16, T), BF),
        vm((2, 32, 16, T), BF),
        vm((T, D), BF),
        vm((3, T, KV), BF),
        vm((3, T, KV), BF),
        vm((2, T, KV), BF),
        vm((2, T, KV), BF),
        vm((2 * T, D), BF),
        vm((8, 2, 16, D), BF),
        vm((8, 8, 2, 16, 128), BF),
        vm((7, 2, 16, D), BF),
        vm((7, 8, 2, 16, 128), BF),
        vm((8, 2, 16, 128), BF),
        vm((8, 2, 16, 128), BF),
        vm((7, 2, 16, 128), BF),
        vm((7, 2, 16, 128), BF),
        vm((4, 16, 128), F32),
        vm((7, 16, 128), F32),
        dma((7,)),
        dma((6,)), dma((6,)),
        dma((7,)), dma((7,)),
        dma((6,)), dma((6,)),
        dma((7,)), dma((1,)),
        dma((2,)), dma((2,)),
        dma((4,)), dma((4,)),
        dma((7,)), dma((7,)),
        dma((7,)), dma((7,)),
        dma((7,)), dma((7,)),
        dma((7,)), dma((7,)),
        dma((7,)), dma((7,)),
    ]
    out = pl.pallas_call(
        kernel,
        out_shape=(
            jax.ShapeDtypeStruct((T, D), BF),
            jax.ShapeDtypeStruct((T, D), BF),
            jax.ShapeDtypeStruct((T, KV), BF),
            jax.ShapeDtypeStruct((T, KV), BF),
            jax.ShapeDtypeStruct((16, 64), F32),
        ),
        in_specs=[hbm] * 7,
        out_specs=(hbm,) * 5,
        scratch_shapes=scratch,
        compiler_params=pltpu.CompilerParams(
            collective_id=0, has_side_effects=True, vmem_limit_bytes=VMEM_LIMIT
        ),
        cost_estimate=pl.CostEstimate(
            flops=1_400_000_000, bytes_accessed=1_500_000, transcendentals=400_000
        ),
        name="sublayer",
    )(
        patch_order[0], block_mask[0], queries[0], keys_in[0], values_in[0], out_weight, cotangent[0]
    )
    mixed, gq, gk, gv, gw = pl.pallas_call(
        store,
        out_shape=[jax.ShapeDtypeStruct(o.shape, o.dtype) for o in out],
        in_specs=[hbm] * 5,
        out_specs=[hbm] * 5,
        scratch_shapes=[vm(o.shape, o.dtype) for o in out] + [dma((10,))],
        compiler_params=pltpu.CompilerParams(vmem_limit_bytes=VMEM_LIMIT),
        name="store",
    )(*out)
    return mixed[None], gq[None], gk[None], gv[None], gw


def solution(mesh):
    tokens = P("dp", "ctx", None)
    in_specs = (tokens, tokens, tokens, tokens, tokens, P("dp", None), tokens)
    out_specs = (tokens, tokens, tokens, tokens, P("dp", "ctx"))
    return jax.shard_map(shards, mesh=mesh, in_specs=in_specs, out_specs=out_specs, check_vma=False)
```

```python
import functools
import math

import jax
import jax.numpy as jnp
from jax import lax
from jax.experimental import pallas as pl
from jax.experimental.pallas import tpu as pltpu
from jax.sharding import PartitionSpec as P

MESH = pl.DeviceIdType.MESH
BF = jnp.bfloat16
F32 = jnp.float32
HD = 128
T = 128
D = 1024
GROUP = 4
GROUPS = 2
KV = 256
BLK = 32
VMEM_LIMIT = 60 << 20
D7 = (4, 3, -3, 2, -2, 1, -1)
NT = (((1,), (1,)), ((), ()))
NN = (((1,), (0,)), ((), ()))


def kernel(
    order_h, mask_h, q_h, k_h, v_h, w_h, dy_h,
    mixed_o, gq_o, gk_o, gv_o, gw_o,
    mask_s, order_v, q_v, dy2, kb, vb, order_n, w_full,
    qst, dast, ktr, vtr, st, pf, pb, dsb, att_t, lhs, att,
    part_k, part_v, got_k, got_v,
    dyp, ga, gc, ra1, rc1, ga2, gc2, ra2, rc2, gx, rx,
    loc_sem, halo_ss, halo_rs, wz_ss, wz_rs, wx_ss, wx_rs, wc_ss, wc_rs,
    core_ss, core_rs, ph_ss, ph_rs,
    a1_ss, a1_rs, c1_ss, c1_rs, a2_ss, a2_rs, c2_ss, c2_rs, x_ss, x_rs,
):
    c = lax.axis_index("ctx")
    d = lax.axis_index("dp")
    xh, y = c // 8, c % 8
    z, xl, k = d // 8, (d // 2) % 4, d % 2
    x = xh * 4 + xl

    def dev(x_, y_, z_, k_):
        return ((x_ // 4) * 8 + y_, z_ * 8 + (x_ % 4) * 2 + k_)

    def zdev(s):
        return dev(x, y, (z + s + 8) % 8, k)

    def xdev(s):
        return dev((x + s + 8) % 8, y, z, k)

    def ydev(s):
        return dev(x, (y + s + 8) % 8, z, k)

    def cdev(s):
        return ((c + s + 16) % 16, d)

    other = 1 - k
    mate = dev(x, y, z, other)

    def rcopy(src, dst, ss, rs, to):
        return pltpu.make_async_remote_copy(
            src_ref=src, dst_ref=dst, send_sem=ss, recv_sem=rs, device_id=to, device_id_type=MESH
        )

    loc = [
        pltpu.make_async_copy(q_h, q_v, loc_sem.at[0]),
        pltpu.make_async_copy(k_h, kb.at[1], loc_sem.at[1]),
        pltpu.make_async_copy(v_h, vb.at[1], loc_sem.at[2]),
        pltpu.make_async_copy(dy_h, dy2.at[0], loc_sem.at[3]),
        pltpu.make_async_copy(w_h, w_full.at[z, xl, k], loc_sem.at[4]),
        pltpu.make_async_copy(order_h, order_v, loc_sem.at[5]),
        pltpu.make_async_copy(mask_h, mask_s, loc_sem.at[6]),
    ]
    for cp in loc:
        cp.start()

    bar = pltpu.get_barrier_semaphore()
    friends = [cdev(1), cdev(-1), mate]
    for s in D7:
        friends += [zdev(s), xdev(s), ydev(s)]
    for f in friends:
        pl.semaphore_signal(bar, inc=1, device_id=f, device_id_type=MESH)
    loc[5].wait()
    loc[6].wait()
    pl.semaphore_wait(bar, len(friends))

    sends = []
    def go(cp):
        cp.start()
        sends.append(cp)
        return cp

    halo, halo_v = [], []
    sides = ((1, 0), (-1, 2))
    for i, (s, slot) in enumerate(sides):
        halo.append(go(rcopy(k_h, kb.at[slot], halo_ss.at[3 * i], halo_rs.at[3 * i], cdev(s))))
        halo.append(go(rcopy(order_h, order_n.at[i], halo_ss.at[3 * i + 2], halo_rs.at[3 * i + 2], cdev(s))))
    for i, (s, slot) in enumerate(sides):
        halo_v.append(go(rcopy(v_h, vb.at[slot], halo_ss.at[3 * i + 1], halo_rs.at[3 * i + 1], cdev(s))))
    for i, s in enumerate(D7):
        go(rcopy(w_h, w_full.at[z, xl, k], wz_ss.at[i], wz_rs.at[i], zdev(s)))
    dy_c = go(rcopy(dy_h, dy2.at[1], core_ss.at[0], core_rs.at[0], mate))

    for cp in loc[:3]:
        cp.wait()
    for h in range(8):
        qst[h * T : (h + 1) * T, :] = q_v[:, h * HD : (h + 1) * HD]
    for g in range(GROUPS):
        st[g, T : 2 * T, :] = lax.dot_general(
            kb[1, :, g * HD : (g + 1) * HD], qst[g * 512 : (g + 1) * 512, :], NT,
            preferred_element_type=F32,
        )
    jcol = lax.broadcasted_iota(jnp.int32, (T, T), 1)
    irow = lax.broadcasted_iota(jnp.int32, (T, T), 0)
    jblk = jcol // BLK

    def key_block(order):
        hit = irow == jnp.broadcast_to(order, (T, T))
        return jnp.sum(jnp.where(hit, jblk, 0).astype(F32), axis=1, keepdims=True)

    own_hit = (irow == jnp.broadcast_to(order_v[...], (T, T))).astype(F32).astype(BF)
    jrow = (lax.broadcasted_iota(jnp.int32, (8, T), 1) // BLK).astype(F32).astype(BF)
    q_block = lax.dot_general(jrow, own_hit, NT, preferred_element_type=F32)[0:1]

    def order_columns(i):
        for y_ in range(8):
            lo = dy2[i, :, y_ * 64 : y_ * 64 + 64]
            hi = dy2[i, :, 512 + y_ * 64 : 576 + y_ * 64]
            dyp[i * T : (i + 1) * T, y_ * 128 : (y_ + 1) * 128] = jnp.concatenate([lo, hi], axis=1)

    loc[3].wait()
    order_columns(0)

    for cp in halo:
        cp.wait_recv()
    for i, slot in ((0, 0), (1, 2)):
        kblk = key_block(order_n[i])
        allow = jnp.zeros((T, T), F32)
        for b2 in range(4):
            row = jnp.zeros((1, T), F32)
            for b1 in range(4):
                seen = jnp.full((1, T), mask_s[b1, 4 * i + b2], jnp.int32).astype(F32)
                row = row + jnp.where(q_block == float(b1), seen, 0.0)
            allow = allow + jnp.where(kblk == float(b2), jnp.broadcast_to(row, (T, T)), 0.0)
        allow4 = jnp.concatenate([allow] * GROUP, axis=1)
        for g in range(GROUPS):
            s_g = lax.dot_general(
                kb[slot, :, g * HD : (g + 1) * HD], qst[g * 512 : (g + 1) * 512, :], NT,
                preferred_element_type=F32,
            )
            st[g, slot * T : (slot + 1) * T, :] = jnp.where(allow4 > 0.5, s_g, -1e30)
    scale = 1.0 / math.sqrt(HD)
    to_two = scale * math.log2(math.e)
    for g in range(GROUPS):
        top = jnp.max(st[g], axis=0, keepdims=True)
        e = jnp.exp2((st[g] - top) * to_two)
        p = e * (1.0 / jnp.sum(e, axis=0, keepdims=True))
        pf[g] = p
        pb[g] = p.astype(BF)
    for cp in halo_v:
        cp.wait_recv()
    for g in range(GROUPS):
        v_g = vb[:, :, g * HD : (g + 1) * HD].reshape(3 * T, HD)
        vtr[g] = v_g.T
        at = jnp.dot(vtr[g], pb[g], preferred_element_type=F32).astype(BF)
        for j in range(GROUP):
            h = g * GROUP + j
            att_t[h * 4 : (h + 1) * 4] = at[:, j * T : (j + 1) * T].reshape(4, 2, 16, T)
            att[:, h * HD : (h + 1) * HD] = at[:, j * T : (j + 1) * T].T
    a_c = go(rcopy(att_t.at[:, other], lhs.at[1], core_ss.at[1], core_rs.at[1], mate))
    loc[4].wait()
    for i, s in enumerate(D7):
        there = w_full.at[(z - s + 8) % 8, xl, k]
        rcopy(w_h, there, wz_ss.at[i], wz_rs.at[i], zdev(s)).wait_recv()
    legs_w = ((1, 0), (-1, 0), (2, 0), (1, 1), (-1, 1), (-2, 1))
    for i, (s, half) in enumerate(legs_w):
        rows = w_full.at[pl.ds(half * 4, 4), xl, k]
        go(rcopy(rows, rows, wx_ss.at[i], wx_rs.at[i], xdev(s)))
    column = w_full.at[:, xl, k]
    go(rcopy(column, column, wc_ss.at[0], wc_rs.at[0], mate))
    dy_c.wait_recv()
    order_columns(1)
    lhs[0] = att_t[:, k]
    a_c.wait_recv()
    left = jnp.concatenate([lhs[0], lhs[1]], axis=2).reshape(8, 4, 16, 2 * T)
    g_a = jnp.dot(left[:, :2].reshape(256, 2 * T), dyp[...], preferred_element_type=F32)
    ga[...] = g_a.astype(BF).reshape(8, 2, 16, D)
    a1 = []
    for i, s in enumerate(D7):
        a1.append(go(rcopy(ga.at[(z + s + 8) % 8], ra1.at[i], a1_ss.at[i], a1_rs.at[i], zdev(s))))
    g_c = jnp.dot(left[:, 2:].reshape(256, 2 * T), dyp[...], preferred_element_type=F32)
    for y_ in range(8):
        gc[y_] = g_c[:, y_ * 128 : (y_ + 1) * 128].astype(BF).reshape(8, 2, 16, 128)
    c1 = []
    for i, s in enumerate(D7):
        c1.append(go(rcopy(gc.at[(y + s + 8) % 8], rc1.at[i], c1_ss.at[i], c1_rs.at[i], ydev(s))))

    for g in range(GROUPS):
        ktr[g] = kb[:, :, g * HD : (g + 1) * HD].reshape(3 * T, HD).T
    for i, (s, half) in enumerate(legs_w):
        there = w_full.at[pl.ds(half * 4, 4), (xl - s + 4) % 4, k]
        rcopy(there, there, wx_ss.at[i], wx_rs.at[i], xdev(s)).wait_recv()
        go(rcopy(there, there, wc_ss.at[1 + i], wc_rs.at[0], mate))
    there = w_full.at[:, :, other]
    rcopy(there, there, wc_ss.at[0], wc_rs.at[0], mate).wait_recv()
    for h in range(8):
        dast[h * T : (h + 1) * T, :] = lax.dot_general(
            dy2[0], w_full[h].reshape(HD, D), NT, preferred_element_type=F32
        ).astype(BF)
    part = []
    for g in range(GROUPS):
        pv = jnp.dot(pb[g], dast[g * 512 : (g + 1) * 512, :], preferred_element_type=F32)
        part_v[:, :, g * HD : (g + 1) * HD] = pv.astype(BF).reshape(3, T, HD)
    part.append(go(rcopy(part_v.at[0], got_v.at[0], ph_ss.at[0], ph_rs.at[0], cdev(-1))))
    part.append(go(rcopy(part_v.at[2], got_v.at[1], ph_ss.at[1], ph_rs.at[1], cdev(1))))
    for g in range(GROUPS):
        v_g = vb[:, :, g * HD : (g + 1) * HD].reshape(3 * T, HD)
        dp_ = lax.dot_general(
            v_g, dast[g * 512 : (g + 1) * 512, :], NT, preferred_element_type=F32
        )
        delta = jnp.sum(pb[g].astype(F32) * dp_, axis=0, keepdims=True)
        dsb[g] = (pf[g] * (dp_ - delta)).astype(BF)
        pk = jnp.dot(dsb[g], qst[g * 512 : (g + 1) * 512, :], preferred_element_type=F32)
        part_k[:, :, g * HD : (g + 1) * HD] = (pk * scale).astype(BF).reshape(3, T, HD)
    part.append(go(rcopy(part_k.at[0], got_k.at[0], ph_ss.at[2], ph_rs.at[2], cdev(-1))))
    part.append(go(rcopy(part_k.at[2], got_k.at[1], ph_ss.at[3], ph_rs.at[3], cdev(1))))

    for cp in a1:
        cp.wait_recv()
    s_a = ga[z].astype(F32)
    for i in range(7):
        s_a = s_a + ra1[i].astype(F32)
    s_a = s_a.astype(BF)
    for y_ in range(8):
        ga2[y_] = s_a[:, :, y_ * 128 : (y_ + 1) * 128]
    a2 = []
    for i, s in enumerate(D7):
        a2.append(go(rcopy(ga2.at[(y + s + 8) % 8], ra2.at[i], a2_ss.at[i], a2_rs.at[i], ydev(s))))
    for cp in c1:
        cp.wait_recv()
    s_c = gc[y].astype(F32)
    for i in range(7):
        s_c = s_c + rc1[i].astype(F32)
    gc2[...] = s_c.astype(BF)
    c2 = []
    for i, s in enumerate(D7):
        c2.append(go(rcopy(gc2.at[(z + s + 8) % 8], rc2.at[i], c2_ss.at[i], c2_rs.at[i], zdev(s))))

    mixed_o[...] = jnp.dot(
        att[...], w_full[...].reshape(D, D), preferred_element_type=F32
    ).astype(BF)
    for g in range(GROUPS):
        gq = jnp.dot(ktr[g], dsb[g], preferred_element_type=F32) * scale
        for j in range(GROUP):
            h = g * GROUP + j
            gq_o[:, h * HD : (h + 1) * HD] = gq[:, j * T : (j + 1) * T].astype(BF).T

    for cp in a2:
        cp.wait_recv()
    f_a = ga2[y].astype(F32)
    for i in range(7):
        f_a = f_a + ra2[i].astype(F32)
    gx[0:2] = f_a
    for cp in c2:
        cp.wait_recv()
    f_c = gc2[z].astype(F32)
    for i in range(7):
        f_c = f_c + rc2[i].astype(F32)
    gx[2:4] = f_c
    legs = []
    for i, s in enumerate(D7):
        to = (xl + s + 8) % 4
        legs.append(go(rcopy(gx.at[to], rx.at[i], x_ss.at[i], x_rs.at[i], xdev(s))))

    for cp in part:
        cp.wait_recv()
    gv_o[...] = (part_v[1].astype(F32) + got_v[0].astype(F32) + got_v[1].astype(F32)).astype(BF)
    gk_o[...] = (part_k[1].astype(F32) + got_k[0].astype(F32) + got_k[1].astype(F32)).astype(BF)

    for cp in legs:
        cp.wait_recv()
    total = gx[xl]
    for i in range(7):
        total = total + rx[i]
    norm = 1.0 / math.sqrt(64 * 16 * T)
    high = jnp.full((16, 64), xh, jnp.int32) > 0
    gw_o[...] = jnp.where(high, total[:, 64:], total[:, :64]) * norm

    for cp in sends:
        cp.wait_send()


def store(*refs):
    saves = [pltpu.make_async_copy(refs[i], refs[5 + i], refs[10].at[i]) for i in range(5)]
    for cp in saves:
        cp.start()
    for cp in saves:
        cp.wait()


def shards(queries, keys_in, values_in, patch_order, block_mask, out_weight, cotangent):
    dma = pltpu.SemaphoreType.DMA
    vm = pltpu.VMEM
    hbm = pl.BlockSpec(memory_space=pltpu.HBM)
    in_vmem = pl.BlockSpec(memory_space=pltpu.VMEM)
    scratch = [
        pltpu.SMEM((4, 8), jnp.int32),
        vm((1, T), jnp.int32),
        vm((T, D), BF),
        vm((2, T, D), BF),
        vm((3, T, KV), BF),
        vm((3, T, KV), BF),
        vm((2, 1, T), jnp.int32),
        vm((8, 4, 2, 16, D), BF),
        vm((8 * T, HD), BF),
        vm((8 * T, HD), BF),
        vm((GROUPS, HD, 3 * T), BF),
        vm((GROUPS, HD, 3 * T), BF),
        vm((GROUPS, 3 * T, 512), F32),
        vm((GROUPS, 3 * T, 512), F32),
        vm((GROUPS, 3 * T, 512), BF),
        vm((GROUPS, 3 * T, 512), BF),
        vm((32, 2, 16, T), BF),
        vm((2, 32, 16, T), BF),
        vm((T, D), BF),
        vm((3, T, KV), BF),
        vm((3, T, KV), BF),
        vm((2, T, KV), BF),
        vm((2, T, KV), BF),
        vm((2 * T, D), BF),
        vm((8, 2, 16, D), BF),
        vm((8, 8, 2, 16, 128), BF),
        vm((7, 2, 16, D), BF),
        vm((7, 8, 2, 16, 128), BF),
        vm((8, 2, 16, 128), BF),
        vm((8, 2, 16, 128), BF),
        vm((7, 2, 16, 128), BF),
        vm((7, 2, 16, 128), BF),
        vm((4, 16, 128), F32),
        vm((7, 16, 128), F32),
        dma((7,)),
        dma((6,)), dma((6,)),
        dma((7,)), dma((7,)),
        dma((6,)), dma((6,)),
        dma((7,)), dma((1,)),
        dma((2,)), dma((2,)),
        dma((4,)), dma((4,)),
        dma((7,)), dma((7,)),
        dma((7,)), dma((7,)),
        dma((7,)), dma((7,)),
        dma((7,)), dma((7,)),
        dma((7,)), dma((7,)),
    ]
    out = pl.pallas_call(
        kernel,
        out_shape=(
            vm((T, D), BF),
            vm((T, D), BF),
            vm((T, KV), BF),
            vm((T, KV), BF),
            vm((16, 64), F32),
        ),
        in_specs=[hbm] * 7,
        out_specs=(in_vmem,) * 5,
        scratch_shapes=scratch,
        compiler_params=pltpu.CompilerParams(
            collective_id=0, has_side_effects=True, vmem_limit_bytes=VMEM_LIMIT
        ),
        cost_estimate=pl.CostEstimate(
            flops=1_400_000_000, bytes_accessed=1_500_000, transcendentals=400_000
        ),
        name="sublayer",
    )(
        patch_order[0], block_mask[0], queries[0], keys_in[0], values_in[0], out_weight, cotangent[0]
    )
    mixed, gq, gk, gv, gw = pl.pallas_call(
        store,
        out_shape=[jax.ShapeDtypeStruct(o.shape, o.dtype) for o in out],
        in_specs=[in_vmem] * 5,
        out_specs=[hbm] * 5,
        scratch_shapes=[dma((5,))],
        compiler_params=pltpu.CompilerParams(vmem_limit_bytes=4 << 20),
        name="store",
    )(*out)
    return mixed[None], gq[None], gk[None], gv[None], gw


def solution(mesh):
    tokens = P("dp", "ctx", None)
    in_specs = (tokens, tokens, tokens, tokens, tokens, P("dp", None), tokens)
    out_specs = (tokens, tokens, tokens, tokens, P("dp", "ctx"))
    return jax.shard_map(shards, mesh=mesh, in_specs=in_specs, out_specs=out_specs, check_vma=False)
```

```python
import functools
import math

import jax
import jax.numpy as jnp
from jax import lax
from jax.experimental import pallas as pl
from jax.experimental.pallas import tpu as pltpu
from jax.sharding import PartitionSpec as P

MESH = pl.DeviceIdType.MESH
BF = jnp.bfloat16
F32 = jnp.float32
HD = 128
T = 128
D = 1024
GROUP = 4
GROUPS = 2
KV = 256
BLK = 32
VMEM_LIMIT = 60 << 20
D7 = (4, 3, -3, 2, -2, 1, -1)
NEAR_FIRST = (5, 6, 3, 4, 1, 2, 0)
NT = (((1,), (1,)), ((), ()))
NN = (((1,), (0,)), ((), ()))


def kernel(
    order_h, mask_h, q_h, k_h, v_h, w_h, dy_h,
    mixed_o, gq_o, gk_o, gv_o, gw_o,
    mask_s, order_v, q_v, dy2, kb, vb, order_n, w_full,
    qst, dast, ktr, vtr, st, pf, pb, dsb, att_t, lhs, att,
    part_k, part_v, got_k, got_v,
    dyp, ga, gc, ra1, rc1, ga2, gc2, ra2, rc2, gx, rx,
    loc_sem, halo_ss, halo_rs, wz_ss, wz_rs, wx_ss, wx_rs, wc_ss, wc_rs,
    core_ss, core_rs, ph_ss, ph_rs,
    a1_ss, a1_rs, c1_ss, c1_rs, a2_ss, a2_rs, c2_ss, c2_rs, x_ss, x_rs,
):
    c = lax.axis_index("ctx")
    d = lax.axis_index("dp")
    xh, y = c // 8, c % 8
    z, xl, k = d // 8, (d // 2) % 4, d % 2
    x = xh * 4 + xl

    def dev(x_, y_, z_, k_):
        return ((x_ // 4) * 8 + y_, z_ * 8 + (x_ % 4) * 2 + k_)

    def zdev(s):
        return dev(x, y, (z + s + 8) % 8, k)

    def xdev(s):
        return dev((x + s + 8) % 8, y, z, k)

    def ydev(s):
        return dev(x, (y + s + 8) % 8, z, k)

    def cdev(s):
        return ((c + s + 16) % 16, d)

    other = 1 - k
    mate = dev(x, y, z, other)

    def rcopy(src, dst, ss, rs, to):
        return pltpu.make_async_remote_copy(
            src_ref=src, dst_ref=dst, send_sem=ss, recv_sem=rs, device_id=to, device_id_type=MESH
        )

    loc = [
        pltpu.make_async_copy(q_h, q_v, loc_sem.at[0]),
        pltpu.make_async_copy(k_h, kb.at[1], loc_sem.at[1]),
        pltpu.make_async_copy(v_h, vb.at[1], loc_sem.at[2]),
        pltpu.make_async_copy(dy_h, dy2.at[0], loc_sem.at[3]),
        pltpu.make_async_copy(w_h, w_full.at[z, xl, k], loc_sem.at[4]),
        pltpu.make_async_copy(order_h, order_v, loc_sem.at[5]),
        pltpu.make_async_copy(mask_h, mask_s, loc_sem.at[6]),
    ]
    for cp in loc:
        cp.start()

    bar = pltpu.get_barrier_semaphore()
    friends = [cdev(1), cdev(-1), mate]
    for s in D7:
        friends += [zdev(s), xdev(s), ydev(s)]
    for f in friends:
        pl.semaphore_signal(bar, inc=1, device_id=f, device_id_type=MESH)
    loc[5].wait()
    loc[6].wait()
    pl.semaphore_wait(bar, len(friends))

    sends = []
    def go(cp):
        cp.start()
        sends.append(cp)
        return cp

    halo, halo_v = [], []
    sides = ((1, 0), (-1, 2))
    for i, (s, slot) in enumerate(sides):
        halo.append(go(rcopy(k_h, kb.at[slot], halo_ss.at[3 * i], halo_rs.at[3 * i], cdev(s))))
        halo.append(go(rcopy(order_h, order_n.at[i], halo_ss.at[3 * i + 2], halo_rs.at[3 * i + 2], cdev(s))))
    for i, (s, slot) in enumerate(sides):
        halo_v.append(go(rcopy(v_h, vb.at[slot], halo_ss.at[3 * i + 1], halo_rs.at[3 * i + 1], cdev(s))))
    for i, s in enumerate(D7):
        go(rcopy(w_h, w_full.at[z, xl, k], wz_ss.at[i], wz_rs.at[i], zdev(s)))
    dy_c = go(rcopy(dy_h, dy2.at[1], core_ss.at[0], core_rs.at[0], mate))

    for cp in loc[:3]:
        cp.wait()
    for h in range(8):
        qst[h * T : (h + 1) * T, :] = q_v[:, h * HD : (h + 1) * HD]
    for g in range(GROUPS):
        st[g, T : 2 * T, :] = lax.dot_general(
            kb[1, :, g * HD : (g + 1) * HD], qst[g * 512 : (g + 1) * 512, :], NT,
            preferred_element_type=F32,
        )
    jcol = lax.broadcasted_iota(jnp.int32, (T, T), 1)
    irow = lax.broadcasted_iota(jnp.int32, (T, T), 0)
    jblk = jcol // BLK

    def key_block(order):
        hit = irow == jnp.broadcast_to(order, (T, T))
        return jnp.sum(jnp.where(hit, jblk, 0).astype(F32), axis=1, keepdims=True)

    own_hit = (irow == jnp.broadcast_to(order_v[...], (T, T))).astype(F32).astype(BF)
    jrow = (lax.broadcasted_iota(jnp.int32, (8, T), 1) // BLK).astype(F32).astype(BF)
    q_block = lax.dot_general(jrow, own_hit, NT, preferred_element_type=F32)[0:1]

    def order_columns(i):
        for y_ in range(8):
            lo = dy2[i, :, y_ * 64 : y_ * 64 + 64]
            hi = dy2[i, :, 512 + y_ * 64 : 576 + y_ * 64]
            dyp[i * T : (i + 1) * T, y_ * 128 : (y_ + 1) * 128] = jnp.concatenate([lo, hi], axis=1)

    loc[3].wait()
    order_columns(0)

    for cp in halo:
        cp.wait_recv()
    for i, slot in ((0, 0), (1, 2)):
        kblk = key_block(order_n[i])
        allow = jnp.zeros((T, T), F32)
        for b2 in range(4):
            row = jnp.zeros((1, T), F32)
            for b1 in range(4):
                seen = jnp.full((1, T), mask_s[b1, 4 * i + b2], jnp.int32).astype(F32)
                row = row + jnp.where(q_block == float(b1), seen, 0.0)
            allow = allow + jnp.where(kblk == float(b2), jnp.broadcast_to(row, (T, T)), 0.0)
        allow4 = jnp.concatenate([allow] * GROUP, axis=1)
        for g in range(GROUPS):
            s_g = lax.dot_general(
                kb[slot, :, g * HD : (g + 1) * HD], qst[g * 512 : (g + 1) * 512, :], NT,
                preferred_element_type=F32,
            )
            st[g, slot * T : (slot + 1) * T, :] = jnp.where(allow4 > 0.5, s_g, -1e30)
    scale = 1.0 / math.sqrt(HD)
    to_two = scale * math.log2(math.e)
    for g in range(GROUPS):
        top = jnp.max(st[g], axis=0, keepdims=True)
        e = jnp.exp2((st[g] - top) * to_two)
        p = e * (1.0 / jnp.sum(e, axis=0, keepdims=True))
        pf[g] = p
        pb[g] = p.astype(BF)
    for cp in halo_v:
        cp.wait_recv()
    for g in range(GROUPS):
        v_g = vb[:, :, g * HD : (g + 1) * HD].reshape(3 * T, HD)
        vtr[g] = v_g.T
        at = jnp.dot(vtr[g], pb[g], preferred_element_type=F32).astype(BF)
        for j in range(GROUP):
            h = g * GROUP + j
            att_t[h * 4 : (h + 1) * 4] = at[:, j * T : (j + 1) * T].reshape(4, 2, 16, T)
            att[:, h * HD : (h + 1) * HD] = at[:, j * T : (j + 1) * T].T
    a_c = go(rcopy(att_t.at[:, other], lhs.at[1], core_ss.at[1], core_rs.at[1], mate))
    loc[4].wait()
    for i, s in enumerate(D7):
        there = w_full.at[(z - s + 8) % 8, xl, k]
        rcopy(w_h, there, wz_ss.at[i], wz_rs.at[i], zdev(s)).wait_recv()
    legs_w = ((2, 0), (-2, 1), (1, 0), (-1, 0), (1, 1), (-1, 1))
    for i, (s, half) in enumerate(legs_w):
        rows = w_full.at[pl.ds(half * 4, 4), xl, k]
        go(rcopy(rows, rows, wx_ss.at[i], wx_rs.at[i], xdev(s)))
    column = w_full.at[:, xl, k]
    go(rcopy(column, column, wc_ss.at[0], wc_rs.at[0], mate))
    dy_c.wait_recv()
    order_columns(1)
    lhs[0] = att_t[:, k]
    a_c.wait_recv()
    left = jnp.concatenate([lhs[0], lhs[1]], axis=2).reshape(8, 4, 16, 2 * T)
    g_a = jnp.dot(left[:, :2].reshape(256, 2 * T), dyp[...], preferred_element_type=F32)
    ga[...] = g_a.astype(BF).reshape(8, 2, 16, D)
    a1 = []
    for i, s in enumerate(D7):
        a1.append(go(rcopy(ga.at[(z + s + 8) % 8], ra1.at[i], a1_ss.at[i], a1_rs.at[i], zdev(s))))
    g_c = jnp.dot(left[:, 2:].reshape(256, 2 * T), dyp[...], preferred_element_type=F32)
    for y_ in range(8):
        gc[y_] = g_c[:, y_ * 128 : (y_ + 1) * 128].astype(BF).reshape(8, 2, 16, 128)
    c1 = []
    for i, s in enumerate(D7):
        c1.append(go(rcopy(gc.at[(y + s + 8) % 8], rc1.at[i], c1_ss.at[i], c1_rs.at[i], ydev(s))))

    for g in range(GROUPS):
        ktr[g] = kb[:, :, g * HD : (g + 1) * HD].reshape(3 * T, HD).T
    for i, (s, half) in enumerate(legs_w):
        there = w_full.at[pl.ds(half * 4, 4), (xl - s + 4) % 4, k]
        rcopy(there, there, wx_ss.at[i], wx_rs.at[i], xdev(s)).wait_recv()
        go(rcopy(there, there, wc_ss.at[1 + i], wc_rs.at[0], mate))
    there = w_full.at[:, :, other]
    rcopy(there, there, wc_ss.at[0], wc_rs.at[0], mate).wait_recv()
    for h in range(8):
        dast[h * T : (h + 1) * T, :] = lax.dot_general(
            dy2[0], w_full[h].reshape(HD, D), NT, preferred_element_type=F32
        ).astype(BF)
    part = []
    for g in range(GROUPS):
        pv = jnp.dot(pb[g], dast[g * 512 : (g + 1) * 512, :], preferred_element_type=F32)
        part_v[:, :, g * HD : (g + 1) * HD] = pv.astype(BF).reshape(3, T, HD)
    part.append(go(rcopy(part_v.at[0], got_v.at[0], ph_ss.at[0], ph_rs.at[0], cdev(-1))))
    part.append(go(rcopy(part_v.at[2], got_v.at[1], ph_ss.at[1], ph_rs.at[1], cdev(1))))
    for g in range(GROUPS):
        v_g = vb[:, :, g * HD : (g + 1) * HD].reshape(3 * T, HD)
        dp_ = lax.dot_general(
            v_g, dast[g * 512 : (g + 1) * 512, :], NT, preferred_element_type=F32
        )
        delta = jnp.sum(pb[g].astype(F32) * dp_, axis=0, keepdims=True)
        dsb[g] = (pf[g] * (dp_ - delta)).astype(BF)
        pk = jnp.dot(dsb[g], qst[g * 512 : (g + 1) * 512, :], preferred_element_type=F32)
        part_k[:, :, g * HD : (g + 1) * HD] = (pk * scale).astype(BF).reshape(3, T, HD)
    part.append(go(rcopy(part_k.at[0], got_k.at[0], ph_ss.at[2], ph_rs.at[2], cdev(-1))))
    part.append(go(rcopy(part_k.at[2], got_k.at[1], ph_ss.at[3], ph_rs.at[3], cdev(1))))

    s_a = ga[z].astype(F32)
    for i in NEAR_FIRST:
        a1[i].wait_recv()
        s_a = s_a + ra1[i].astype(F32)
    s_a = s_a.astype(BF)
    for y_ in range(8):
        ga2[y_] = s_a[:, :, y_ * 128 : (y_ + 1) * 128]
    a2 = []
    for i, s in enumerate(D7):
        a2.append(go(rcopy(ga2.at[(y + s + 8) % 8], ra2.at[i], a2_ss.at[i], a2_rs.at[i], ydev(s))))
    s_c = gc[y].astype(F32)
    for i in NEAR_FIRST:
        c1[i].wait_recv()
        s_c = s_c + rc1[i].astype(F32)
    gc2[...] = s_c.astype(BF)
    c2 = []
    for i, s in enumerate(D7):
        c2.append(go(rcopy(gc2.at[(z + s + 8) % 8], rc2.at[i], c2_ss.at[i], c2_rs.at[i], zdev(s))))

    mixed_o[...] = jnp.dot(
        att[...], w_full[...].reshape(D, D), preferred_element_type=F32
    ).astype(BF)
    for g in range(GROUPS):
        gq = jnp.dot(ktr[g], dsb[g], preferred_element_type=F32) * scale
        for j in range(GROUP):
            h = g * GROUP + j
            gq_o[:, h * HD : (h + 1) * HD] = gq[:, j * T : (j + 1) * T].astype(BF).T

    f_a = ga2[y].astype(F32)
    for i in NEAR_FIRST:
        a2[i].wait_recv()
        f_a = f_a + ra2[i].astype(F32)
    gx[0:2] = f_a
    f_c = gc2[z].astype(F32)
    for i in NEAR_FIRST:
        c2[i].wait_recv()
        f_c = f_c + rc2[i].astype(F32)
    gx[2:4] = f_c
    legs = []
    for i, s in enumerate(D7):
        to = (xl + s + 8) % 4
        legs.append(go(rcopy(gx.at[to], rx.at[i], x_ss.at[i], x_rs.at[i], xdev(s))))

    for cp in part:
        cp.wait_recv()
    gv_o[...] = (part_v[1].astype(F32) + got_v[0].astype(F32) + got_v[1].astype(F32)).astype(BF)
    gk_o[...] = (part_k[1].astype(F32) + got_k[0].astype(F32) + got_k[1].astype(F32)).astype(BF)

    total = gx[xl]
    for i in NEAR_FIRST:
        legs[i].wait_recv()
        total = total + rx[i]
    norm = 1.0 / math.sqrt(64 * 16 * T)
    high = jnp.full((16, 64), xh, jnp.int32) > 0
    gw_o[...] = jnp.where(high, total[:, 64:], total[:, :64]) * norm

    for cp in sends:
        cp.wait_send()


def store(*refs):
    saves = [pltpu.make_async_copy(refs[i], refs[5 + i], refs[10].at[i]) for i in range(5)]
    for cp in saves:
        cp.start()
    for cp in saves:
        cp.wait()


def shards(queries, keys_in, values_in, patch_order, block_mask, out_weight, cotangent):
    dma = pltpu.SemaphoreType.DMA
    vm = pltpu.VMEM
    hbm = pl.BlockSpec(memory_space=pltpu.HBM)
    in_vmem = pl.BlockSpec(memory_space=pltpu.VMEM)
    scratch = [
        pltpu.SMEM((4, 8), jnp.int32),
        vm((1, T), jnp.int32),
        vm((T, D), BF),
        vm((2, T, D), BF),
        vm((3, T, KV), BF),
        vm((3, T, KV), BF),
        vm((2, 1, T), jnp.int32),
        vm((8, 4, 2, 16, D), BF),
        vm((8 * T, HD), BF),
        vm((8 * T, HD), BF),
        vm((GROUPS, HD, 3 * T), BF),
        vm((GROUPS, HD, 3 * T), BF),
        vm((GROUPS, 3 * T, 512), F32),
        vm((GROUPS, 3 * T, 512), F32),
        vm((GROUPS, 3 * T, 512), BF),
        vm((GROUPS, 3 * T, 512), BF),
        vm((32, 2, 16, T), BF),
        vm((2, 32, 16, T), BF),
        vm((T, D), BF),
        vm((3, T, KV), BF),
        vm((3, T, KV), BF),
        vm((2, T, KV), BF),
        vm((2, T, KV), BF),
        vm((2 * T, D), BF),
        vm((8, 2, 16, D), BF),
        vm((8, 8, 2, 16, 128), BF),
        vm((7, 2, 16, D), BF),
        vm((7, 8, 2, 16, 128), BF),
        vm((8, 2, 16, 128), BF),
        vm((8, 2, 16, 128), BF),
        vm((7, 2, 16, 128), BF),
        vm((7, 2, 16, 128), BF),
        vm((4, 16, 128), F32),
        vm((7, 16, 128), F32),
        dma((7,)),
        dma((6,)), dma((6,)),
        dma((7,)), dma((7,)),
        dma((6,)), dma((6,)),
        dma((7,)), dma((1,)),
        dma((2,)), dma((2,)),
        dma((4,)), dma((4,)),
        dma((7,)), dma((7,)),
        dma((7,)), dma((7,)),
        dma((7,)), dma((7,)),
        dma((7,)), dma((7,)),
        dma((7,)), dma((7,)),
    ]
    out = pl.pallas_call(
        kernel,
        out_shape=(
            vm((T, D), BF),
            vm((T, D), BF),
            vm((T, KV), BF),
            vm((T, KV), BF),
            vm((16, 64), F32),
        ),
        in_specs=[hbm] * 7,
        out_specs=(in_vmem,) * 5,
        scratch_shapes=scratch,
        compiler_params=pltpu.CompilerParams(
            collective_id=0, has_side_effects=True, vmem_limit_bytes=VMEM_LIMIT
        ),
        cost_estimate=pl.CostEstimate(
            flops=1_400_000_000, bytes_accessed=1_500_000, transcendentals=400_000
        ),
        name="sublayer",
    )(
        patch_order[0], block_mask[0], queries[0], keys_in[0], values_in[0], out_weight, cotangent[0]
    )
    mixed, gq, gk, gv, gw = pl.pallas_call(
        store,
        out_shape=[jax.ShapeDtypeStruct(o.shape, o.dtype) for o in out],
        in_specs=[in_vmem] * 5,
        out_specs=[hbm] * 5,
        scratch_shapes=[dma((5,))],
        compiler_params=pltpu.CompilerParams(vmem_limit_bytes=4 << 20),
        name="store",
    )(*out)
    return mixed[None], gq[None], gk[None], gv[None], gw


def solution(mesh):
    tokens = P("dp", "ctx", None)
    in_specs = (tokens, tokens, tokens, tokens, tokens, P("dp", None), tokens)
    out_specs = (tokens, tokens, tokens, tokens, P("dp", "ctx"))
    return jax.shard_map(shards, mesh=mesh, in_specs=in_specs, out_specs=out_specs, check_vma=False)
```

```python
import functools
import math

import jax
import jax.numpy as jnp
from jax import lax
from jax.experimental import pallas as pl
from jax.experimental.pallas import tpu as pltpu
from jax.sharding import PartitionSpec as P

MESH = pl.DeviceIdType.MESH
BF = jnp.bfloat16
F32 = jnp.float32
HD = 128
T = 128
D = 1024
GROUP = 4
GROUPS = 2
KV = 256
BLK = 32
VMEM_LIMIT = 60 << 20
D7 = (4, 3, -3, 2, -2, 1, -1)
NEAR_FIRST = (5, 6, 3, 4, 1, 2, 0)
NT = (((1,), (1,)), ((), ()))
NN = (((1,), (0,)), ((), ()))


def kernel(
    order_h, mask_h, q_h, k_h, v_h, w_h, dy_h,
    mixed_o, gq_o, gk_o, gv_o, gw_o,
    mask_s, order_v, q_v, dy2, kb, vb, order_n, w_full,
    qst, dast, ktr, vtr, st, pf, pb, dsb, att_t, lhs, att,
    part_k, part_v, got_k, got_v,
    dyp, ga, gc, ra1, rc1, ga2, gc2, ra2, rc2, gx, rx,
    loc_sem, halo_ss, halo_rs, wz_ss, wz_rs, wx_ss, wx_rs, wc_ss, wc_rs,
    core_ss, core_rs, ph_ss, ph_rs,
    a1_ss, a1_rs, c1_ss, c1_rs, a2_ss, a2_rs, c2_ss, c2_rs, x_ss, x_rs,
):
    c = lax.axis_index("ctx")
    d = lax.axis_index("dp")
    xh, y = c // 8, c % 8
    z, xl, k = d // 8, (d // 2) % 4, d % 2
    x = xh * 4 + xl

    def dev(x_, y_, z_, k_):
        return ((x_ // 4) * 8 + y_, z_ * 8 + (x_ % 4) * 2 + k_)

    def zdev(s):
        return dev(x, y, (z + s + 8) % 8, k)

    def xdev(s):
        return dev((x + s + 8) % 8, y, z, k)

    def ydev(s):
        return dev(x, (y + s + 8) % 8, z, k)

    def cdev(s):
        return ((c + s + 16) % 16, d)

    other = 1 - k
    mate = dev(x, y, z, other)

    def rcopy(src, dst, ss, rs, to):
        return pltpu.make_async_remote_copy(
            src_ref=src, dst_ref=dst, send_sem=ss, recv_sem=rs, device_id=to, device_id_type=MESH
        )

    loc = [
        pltpu.make_async_copy(q_h, q_v, loc_sem.at[0]),
        pltpu.make_async_copy(k_h, kb.at[1], loc_sem.at[1]),
        pltpu.make_async_copy(v_h, vb.at[1], loc_sem.at[2]),
        pltpu.make_async_copy(dy_h, dy2.at[0], loc_sem.at[3]),
        pltpu.make_async_copy(w_h, w_full.at[z, xl, k], loc_sem.at[4]),
        pltpu.make_async_copy(order_h, order_v, loc_sem.at[5]),
        pltpu.make_async_copy(mask_h, mask_s, loc_sem.at[6]),
    ]
    for cp in loc:
        cp.start()

    bar = pltpu.get_barrier_semaphore()
    friends = []
    for s in D7:
        friends += [zdev(s), xdev(s), ydev(s)]
    friends += [cdev(1), cdev(-1), mate]
    for f in friends:
        pl.semaphore_signal(bar, inc=1, device_id=f, device_id_type=MESH)
    loc[5].wait()
    loc[6].wait()
    pl.semaphore_wait(bar, len(friends))

    sends = []
    def go(cp):
        cp.start()
        sends.append(cp)
        return cp

    halo, halo_v = [], []
    sides = ((1, 0), (-1, 2))
    for i, (s, slot) in enumerate(sides):
        halo.append(go(rcopy(k_h, kb.at[slot], halo_ss.at[3 * i], halo_rs.at[3 * i], cdev(s))))
        halo.append(go(rcopy(order_h, order_n.at[i], halo_ss.at[3 * i + 2], halo_rs.at[3 * i + 2], cdev(s))))
    for i, (s, slot) in enumerate(sides):
        halo_v.append(go(rcopy(v_h, vb.at[slot], halo_ss.at[3 * i + 1], halo_rs.at[3 * i + 1], cdev(s))))
    for i, s in enumerate(D7):
        go(rcopy(w_h, w_full.at[z, xl, k], wz_ss.at[i], wz_rs.at[i], zdev(s)))
    dy_c = go(rcopy(dy_h, dy2.at[1], core_ss.at[0], core_rs.at[0], mate))

    for cp in loc[:3]:
        cp.wait()
    for h in range(8):
        qst[h * T : (h + 1) * T, :] = q_v[:, h * HD : (h + 1) * HD]
    for g in range(GROUPS):
        st[g, T : 2 * T, :] = lax.dot_general(
            kb[1, :, g * HD : (g + 1) * HD], qst[g * 512 : (g + 1) * 512, :], NT,
            preferred_element_type=F32,
        )
    jcol = lax.broadcasted_iota(jnp.int32, (T, T), 1)
    irow = lax.broadcasted_iota(jnp.int32, (T, T), 0)
    jblk = jcol // BLK

    def key_block(order):
        hit = irow == jnp.broadcast_to(order, (T, T))
        return jnp.sum(jnp.where(hit, jblk, 0).astype(F32), axis=1, keepdims=True)

    own_hit = (irow == jnp.broadcast_to(order_v[...], (T, T))).astype(F32).astype(BF)
    jrow = (lax.broadcasted_iota(jnp.int32, (8, T), 1) // BLK).astype(F32).astype(BF)
    q_block = lax.dot_general(jrow, own_hit, NT, preferred_element_type=F32)[0:1]

    def order_columns(i):
        for y_ in range(8):
            lo = dy2[i, :, y_ * 64 : y_ * 64 + 64]
            hi = dy2[i, :, 512 + y_ * 64 : 576 + y_ * 64]
            dyp[i * T : (i + 1) * T, y_ * 128 : (y_ + 1) * 128] = jnp.concatenate([lo, hi], axis=1)

    loc[3].wait()
    order_columns(0)

    for cp in halo:
        cp.wait_recv()
    for i, slot in ((0, 0), (1, 2)):
        kblk = key_block(order_n[i])
        allow = jnp.zeros((T, T), F32)
        for b2 in range(4):
            row = jnp.zeros((1, T), F32)
            for b1 in range(4):
                seen = jnp.full((1, T), mask_s[b1, 4 * i + b2], jnp.int32).astype(F32)
                row = row + jnp.where(q_block == float(b1), seen, 0.0)
            allow = allow + jnp.where(kblk == float(b2), jnp.broadcast_to(row, (T, T)), 0.0)
        allow4 = jnp.concatenate([allow] * GROUP, axis=1)
        for g in range(GROUPS):
            s_g = lax.dot_general(
                kb[slot, :, g * HD : (g + 1) * HD], qst[g * 512 : (g + 1) * 512, :], NT,
                preferred_element_type=F32,
            )
            st[g, slot * T : (slot + 1) * T, :] = jnp.where(allow4 > 0.5, s_g, -1e30)
    scale = 1.0 / math.sqrt(HD)
    to_two = scale * math.log2(math.e)
    for g in range(GROUPS):
        top = jnp.max(st[g], axis=0, keepdims=True)
        e = jnp.exp2((st[g] - top) * to_two)
        p = e * (1.0 / jnp.sum(e, axis=0, keepdims=True))
        pf[g] = p
        pb[g] = p.astype(BF)
    for cp in halo_v:
        cp.wait_recv()
    a_c = []
    for g in range(GROUPS):
        v_g = vb[:, :, g * HD : (g + 1) * HD].reshape(3 * T, HD)
        vtr[g] = v_g.T
        at = jnp.dot(vtr[g], pb[g], preferred_element_type=F32).astype(BF)
        for j in range(GROUP):
            h = g * GROUP + j
            att_t[h * 4 : (h + 1) * 4] = at[:, j * T : (j + 1) * T].reshape(4, 2, 16, T)
            att[:, h * HD : (h + 1) * HD] = at[:, j * T : (j + 1) * T].T
        heads = pl.ds(g * 16, 16)
        to_mate = rcopy(
            att_t.at[heads, other], lhs.at[1, heads], core_ss.at[1 + g], core_rs.at[1 + g], mate
        )
        a_c.append(go(to_mate))
    loc[4].wait()
    for i, s in enumerate(D7):
        there = w_full.at[(z - s + 8) % 8, xl, k]
        rcopy(w_h, there, wz_ss.at[i], wz_rs.at[i], zdev(s)).wait_recv()
    legs_w = ((2, 0), (-2, 1), (1, 0), (-1, 0), (1, 1), (-1, 1))
    for i, (s, half) in enumerate(legs_w):
        rows = w_full.at[pl.ds(half * 4, 4), xl, k]
        go(rcopy(rows, rows, wx_ss.at[i], wx_rs.at[i], xdev(s)))
    column = w_full.at[:, xl, k]
    go(rcopy(column, column, wc_ss.at[0], wc_rs.at[0], mate))
    dy_c.wait_recv()
    order_columns(1)
    lhs[0] = att_t[:, k]
    for cp in a_c:
        cp.wait_recv()
    left = jnp.concatenate([lhs[0], lhs[1]], axis=2).reshape(8, 4, 16, 2 * T)
    g_a = jnp.dot(left[:, :2].reshape(256, 2 * T), dyp[...], preferred_element_type=F32)
    ga[...] = g_a.astype(BF).reshape(8, 2, 16, D)
    a1 = []
    for i, s in enumerate(D7):
        a1.append(go(rcopy(ga.at[(z + s + 8) % 8], ra1.at[i], a1_ss.at[i], a1_rs.at[i], zdev(s))))
    g_c = jnp.dot(left[:, 2:].reshape(256, 2 * T), dyp[...], preferred_element_type=F32)
    for y_ in range(8):
        gc[y_] = g_c[:, y_ * 128 : (y_ + 1) * 128].astype(BF).reshape(8, 2, 16, 128)
    c1 = []
    for i, s in enumerate(D7):
        c1.append(go(rcopy(gc.at[(y + s + 8) % 8], rc1.at[i], c1_ss.at[i], c1_rs.at[i], ydev(s))))

    for g in range(GROUPS):
        ktr[g] = kb[:, :, g * HD : (g + 1) * HD].reshape(3 * T, HD).T
    for i, (s, half) in enumerate(legs_w):
        there = w_full.at[pl.ds(half * 4, 4), (xl - s + 4) % 4, k]
        rcopy(there, there, wx_ss.at[i], wx_rs.at[i], xdev(s)).wait_recv()
        go(rcopy(there, there, wc_ss.at[1 + i], wc_rs.at[0], mate))
    there = w_full.at[:, :, other]
    rcopy(there, there, wc_ss.at[0], wc_rs.at[0], mate).wait_recv()
    for h in range(8):
        dast[h * T : (h + 1) * T, :] = lax.dot_general(
            dy2[0], w_full[h].reshape(HD, D), NT, preferred_element_type=F32
        ).astype(BF)
    part = []
    for g in range(GROUPS):
        pv = jnp.dot(pb[g], dast[g * 512 : (g + 1) * 512, :], preferred_element_type=F32)
        part_v[:, :, g * HD : (g + 1) * HD] = pv.astype(BF).reshape(3, T, HD)
    part.append(go(rcopy(part_v.at[0], got_v.at[0], ph_ss.at[0], ph_rs.at[0], cdev(-1))))
    part.append(go(rcopy(part_v.at[2], got_v.at[1], ph_ss.at[1], ph_rs.at[1], cdev(1))))
    for g in range(GROUPS):
        v_g = vb[:, :, g * HD : (g + 1) * HD].reshape(3 * T, HD)
        dp_ = lax.dot_general(
            v_g, dast[g * 512 : (g + 1) * 512, :], NT, preferred_element_type=F32
        )
        delta = jnp.sum(pb[g].astype(F32) * dp_, axis=0, keepdims=True)
        dsb[g] = (pf[g] * (dp_ - delta)).astype(BF)
        pk = jnp.dot(dsb[g], qst[g * 512 : (g + 1) * 512, :], preferred_element_type=F32)
        part_k[:, :, g * HD : (g + 1) * HD] = (pk * scale).astype(BF).reshape(3, T, HD)
    part.append(go(rcopy(part_k.at[0], got_k.at[0], ph_ss.at[2], ph_rs.at[2], cdev(-1))))
    part.append(go(rcopy(part_k.at[2], got_k.at[1], ph_ss.at[3], ph_rs.at[3], cdev(1))))

    s_a = ga[z].astype(F32)
    for i in NEAR_FIRST:
        a1[i].wait_recv()
        s_a = s_a + ra1[i].astype(F32)
    s_a = s_a.astype(BF)
    for y_ in range(8):
        ga2[y_] = s_a[:, :, y_ * 128 : (y_ + 1) * 128]
    a2 = []
    for i, s in enumerate(D7):
        a2.append(go(rcopy(ga2.at[(y + s + 8) % 8], ra2.at[i], a2_ss.at[i], a2_rs.at[i], ydev(s))))
    s_c = gc[y].astype(F32)
    for i in NEAR_FIRST:
        c1[i].wait_recv()
        s_c = s_c + rc1[i].astype(F32)
    gc2[...] = s_c.astype(BF)
    c2 = []
    for i, s in enumerate(D7):
        c2.append(go(rcopy(gc2.at[(z + s + 8) % 8], rc2.at[i], c2_ss.at[i], c2_rs.at[i], zdev(s))))

    mixed_o[...] = jnp.dot(
        att[...], w_full[...].reshape(D, D), preferred_element_type=F32
    ).astype(BF)
    for g in range(GROUPS):
        gq = jnp.dot(ktr[g], dsb[g], preferred_element_type=F32) * scale
        for j in range(GROUP):
            h = g * GROUP + j
            gq_o[:, h * HD : (h + 1) * HD] = gq[:, j * T : (j + 1) * T].astype(BF).T

    f_a = ga2[y].astype(F32)
    for i in NEAR_FIRST:
        a2[i].wait_recv()
        f_a = f_a + ra2[i].astype(F32)
    gx[0:2] = f_a
    f_c = gc2[z].astype(F32)
    for i in NEAR_FIRST:
        c2[i].wait_recv()
        f_c = f_c + rc2[i].astype(F32)
    gx[2:4] = f_c
    legs = []
    for i, s in enumerate(D7):
        to = (xl + s + 8) % 4
        legs.append(go(rcopy(gx.at[to], rx.at[i], x_ss.at[i], x_rs.at[i], xdev(s))))

    for cp in part:
        cp.wait_recv()
    gv_o[...] = (part_v[1].astype(F32) + got_v[0].astype(F32) + got_v[1].astype(F32)).astype(BF)
    gk_o[...] = (part_k[1].astype(F32) + got_k[0].astype(F32) + got_k[1].astype(F32)).astype(BF)

    total = gx[xl]
    for i in NEAR_FIRST:
        legs[i].wait_recv()
        total = total + rx[i]
    norm = 1.0 / math.sqrt(64 * 16 * T)
    high = jnp.full((16, 64), xh, jnp.int32) > 0
    gw_o[...] = jnp.where(high, total[:, 64:], total[:, :64]) * norm

    for cp in sends:
        cp.wait_send()


def store(*refs):
    saves = [pltpu.make_async_copy(refs[i], refs[5 + i], refs[10].at[i]) for i in range(5)]
    for cp in saves:
        cp.start()
    for cp in saves:
        cp.wait()


def shards(queries, keys_in, values_in, patch_order, block_mask, out_weight, cotangent):
    dma = pltpu.SemaphoreType.DMA
    vm = pltpu.VMEM
    hbm = pl.BlockSpec(memory_space=pltpu.HBM)
    in_vmem = pl.BlockSpec(memory_space=pltpu.VMEM)
    scratch = [
        pltpu.SMEM((4, 8), jnp.int32),
        vm((1, T), jnp.int32),
        vm((T, D), BF),
        vm((2, T, D), BF),
        vm((3, T, KV), BF),
        vm((3, T, KV), BF),
        vm((2, 1, T), jnp.int32),
        vm((8, 4, 2, 16, D), BF),
        vm((8 * T, HD), BF),
        vm((8 * T, HD), BF),
        vm((GROUPS, HD, 3 * T), BF),
        vm((GROUPS, HD, 3 * T), BF),
        vm((GROUPS, 3 * T, 512), F32),
        vm((GROUPS, 3 * T, 512), F32),
        vm((GROUPS, 3 * T, 512), BF),
        vm((GROUPS, 3 * T, 512), BF),
        vm((32, 2, 16, T), BF),
        vm((2, 32, 16, T), BF),
        vm((T, D), BF),
        vm((3, T, KV), BF),
        vm((3, T, KV), BF),
        vm((2, T, KV), BF),
        vm((2, T, KV), BF),
        vm((2 * T, D), BF),
        vm((8, 2, 16, D), BF),
        vm((8, 8, 2, 16, 128), BF),
        vm((7, 2, 16, D), BF),
        vm((7, 8, 2, 16, 128), BF),
        vm((8, 2, 16, 128), BF),
        vm((8, 2, 16, 128), BF),
        vm((7, 2, 16, 128), BF),
        vm((7, 2, 16, 128), BF),
        vm((4, 16, 128), F32),
        vm((7, 16, 128), F32),
        dma((7,)),
        dma((6,)), dma((6,)),
        dma((7,)), dma((7,)),
        dma((6,)), dma((6,)),
        dma((7,)), dma((1,)),
        dma((3,)), dma((3,)),
        dma((4,)), dma((4,)),
        dma((7,)), dma((7,)),
        dma((7,)), dma((7,)),
        dma((7,)), dma((7,)),
        dma((7,)), dma((7,)),
        dma((7,)), dma((7,)),
    ]
    out = pl.pallas_call(
        kernel,
        out_shape=(
            vm((T, D), BF),
            vm((T, D), BF),
            vm((T, KV), BF),
            vm((T, KV), BF),
            vm((16, 64), F32),
        ),
        in_specs=[hbm] * 7,
        out_specs=(in_vmem,) * 5,
        scratch_shapes=scratch,
        compiler_params=pltpu.CompilerParams(
            collective_id=0, has_side_effects=True, vmem_limit_bytes=VMEM_LIMIT
        ),
        cost_estimate=pl.CostEstimate(
            flops=1_400_000_000, bytes_accessed=1_500_000, transcendentals=400_000
        ),
        name="sublayer",
    )(
        patch_order[0], block_mask[0], queries[0], keys_in[0], values_in[0], out_weight, cotangent[0]
    )
    mixed, gq, gk, gv, gw = pl.pallas_call(
        store,
        out_shape=[jax.ShapeDtypeStruct(o.shape, o.dtype) for o in out],
        in_specs=[in_vmem] * 5,
        out_specs=[hbm] * 5,
        scratch_shapes=[dma((5,))],
        compiler_params=pltpu.CompilerParams(vmem_limit_bytes=4 << 20),
        name="store",
    )(*out)
    return mixed[None], gq[None], gk[None], gv[None], gw


def solution(mesh):
    tokens = P("dp", "ctx", None)
    in_specs = (tokens, tokens, tokens, tokens, tokens, P("dp", None), tokens)
    out_specs = (tokens, tokens, tokens, tokens, P("dp", "ctx"))
    return jax.shard_map(shards, mesh=mesh, in_specs=in_specs, out_specs=out_specs, check_vma=False)
```
